128 devices in a mesh: sub: 16 (over y, z), corner: 8 (over x, core).
Axes of the slice: x: 4, y: 4, z: 4, core: 2. Of those that a mesh axis runs over, the one named last changes fastest.
Arguments:
- right_side: float32 [2048, 64, 128], P(('sub', 'corner'))
- diagonal: float32 [2048, 64], P(('sub', 'corner')), may hold values from 1.25 to 2.5
- stiffness: float32 [2048, 64, 192], P(('sub', 'corner')), may hold values from -0.035721725 to 0.035721725
- column_index: int32 [2048, 3], P(('sub', 'corner')), may hold values from 0 to 15, as said below
- neighbours: int32 [128, 8], P(('sub', 'corner')), may hold values from 0 to 15, as said below
- face_count: int32 [128, 8], P(('sub', 'corner')), may hold values from 1 to 2, as said below
- corner_group: int32 [128, 8], P(('sub', 'corner')), may hold values from 0 to 15
- coarse_inverse: float32 [1024, 1024], P('corner'), as said below
Outputs:
- solution: float32 [2048, 64, 128], P(('sub', 'corner'))
- residual: float32 [2048, 64, 128], P(('sub', 'corner'))
The draws below stay inside these ranges and needn't reach their ends.
Inputs may be any that keep to these rules, and one draw needn't show every extreme that they name: `neighbours`: for each round r < 8 and corner index c, the subdomains s * 8 + c pair up: if the entry of s is p, then p differs from s and the entry of p in round r is s; the rounds of one subdomain name different partners. `face_count`: equal on both sides of a pair in a round; in every round and corner index some pair shares 2 blocks. `column_index`: the 3 entries of a block row name blocks of the same subdomain other than the row's own, all different; for each k < 3, entry k over the 16 rows of one subdomain names each of its blocks exactly once. `coarse_inverse`: symmetric and positive definite.
All inputs are finite; a program needn't handle non-finite values.
Results may differ from the reference program's by a relative error of at most 0.0003.
Values sent between devices are 32-bit elements; how exact they have to be, the bound alone decides.
No kernel may reach another device: no remote copies, remote signals or barrier semaphores. Data moves between devices by JAX's collectives and lax.ppermute only.
A program may use at most 128 MiB of HBM per device.

```python
import math
import jax
import jax.numpy as jnp
from jax import lax

BLOCK = 64
NB = 16
RHS = 128
BW = 3
FMAX = 2
NCB = 8
NG = 16
DEGREE = 8
ITERS = 3
NNB = 8
SUBDOMS = 128
NCO = 1024
N_SUB = 16
N_CORNER = 8


COARSE_DIAGONAL = 0.05


STIFF_SPREAD = 0.7


def pairing_tables(key):
    subkeys = jax.random.split(jax.random.fold_in(key, 17), 2)
    group_keys = jax.random.split(subkeys[0], N_CORNER)

    def group_masks(group_key):
        return jax.random.permutation(group_key, N_SUB - 1)[:NNB] + 1
    xor_masks = jax.vmap(group_masks)(group_keys).astype(jnp.int32)
    device_ids = jnp.arange(SUBDOMS, dtype=jnp.int32)
    sub_ids = device_ids // N_CORNER
    column_ids = device_ids % N_CORNER
    partners = jnp.bitwise_xor(sub_ids[:, None], xor_masks[column_ids]).astype(jnp.int32)
    lower_sub = jnp.minimum(sub_ids[:, None], partners)
    count_draws = jax.random.randint(subkeys[1], (N_SUB, N_CORNER, NNB), 1, FMAX + 1)
    counts = count_draws[lower_sub, column_ids[:, None], jnp.arange(NNB, dtype=jnp.int32)[None, :]]
    counts = jnp.where(lower_sub == 0, FMAX, counts).astype(jnp.int32)
    return (partners, counts)


def draw_neighbours(key, part):
    partners, counts = pairing_tables(key)
    return partners


def draw_face_count(key, part):
    partners, counts = pairing_tables(key)
    return counts


def draw_column_index(key, part):
    key = jax.random.fold_in(key, 5)
    subkeys = jax.random.split(key, SUBDOMS)

    def one_subdomain(sub_key):
        ordering = jax.random.permutation(sub_key, NB).astype(jnp.int32)
        position = jnp.argsort(ordering).astype(jnp.int32)
        shifts = jnp.arange(1, BW + 1, dtype=jnp.int32)
        return ordering[(position[:, None] + shifts[None, :]) % NB]
    return jax.vmap(one_subdomain)(subkeys).reshape(SUBDOMS * NB, BW).astype(jnp.int32)


def draw_coarse_inverse(key, part):
    key = jax.random.fold_in(key, 7)
    random_part = jax.random.uniform(key, (NCO, NCO), jnp.float32, -1.0, 1.0)
    symmetric = 0.5 * (random_part + random_part.T)
    spread = 0.8 * COARSE_DIAGONAL / NCO
    return COARSE_DIAGONAL * jnp.eye(NCO, dtype=jnp.float32) + spread * symmetric


def draw_stiffness(key, part):
    key = jax.random.fold_in(key, 11)
    entry_bound = STIFF_SPREAD / (2.0 * BW * BLOCK) ** 0.5
    uniform_part = jax.random.uniform(key, (SUBDOMS * NB, BLOCK, BW * BLOCK), jnp.float32, -1.0, 1.0)
    values = entry_bound * uniform_part
    return values


def draw_right_side(key, part):
    key = jax.random.fold_in(key, 3)
    row_count = SUBDOMS * NB
    subdomain_ids = (jnp.arange(row_count, dtype=jnp.int32) // NB).astype(jnp.float32)
    levels = 3.0 ** (subdomain_ids / (SUBDOMS - 1))
    values = jax.random.normal(key, (row_count, BLOCK, RHS), jnp.float32)
    return values * levels[:, None, None]


def set_ends(values, own_key, least, high):
    extent = values.shape
    index_at = [jax.random.randint(jax.random.fold_in(own_key, axis), (), 0, extent[axis]) for axis in range(len(extent))]
    values = values.at[tuple(index_at)].set(least)
    longest = extent.index(max(extent))
    index_at[longest] = (index_at[longest] + 1) % extent[longest]
    return values.at[tuple(index_at)].set(high)


def block_levels(own_key, shape, pieces, least, high):
    factor_of = 1.0
    for dim, blocks in pieces:
        draws = jax.random.uniform(jax.random.fold_in(jax.random.fold_in(own_key, 6), dim), (blocks,), jnp.float32, least / len(pieces), high / len(pieces))
        factor_of = factor_of * jnp.repeat(jnp.exp(draws), shape[dim] // blocks).reshape((-1,) + (1,) * (len(shape) - 1 - dim))
    return factor_of


def setup_inputs(seed: int = 0) -> dict:
    keys = jax.random.split(jax.random.key(seed), 9)
    return {
        "right_side": draw_right_side(jax.random.fold_in(keys[8], 71), 0),
        "diagonal": jnp.clip(jnp.exp(math.log(2.5) - 0.6931472 * jax.random.uniform(keys[1], (SUBDOMS * NB, BLOCK), jnp.float32) ** block_levels(keys[1], (SUBDOMS * NB, BLOCK), ((0, 128),), -0.2, 0.2)), 1.25, 2.5),
        "stiffness": draw_stiffness(jax.random.fold_in(keys[8], 71), 0),
        "column_index": draw_column_index(jax.random.fold_in(keys[8], 71), 0),
        "neighbours": draw_neighbours(jax.random.fold_in(keys[8], 71), 0),
        "face_count": draw_face_count(jax.random.fold_in(keys[8], 71), 0),
        "corner_group": set_ends(jax.random.randint(keys[6], (SUBDOMS, NCB), 0, NG), jax.random.fold_in(keys[6], 1), 0, NG - 1).astype(jnp.int32),
        "coarse_inverse": draw_coarse_inverse(jax.random.fold_in(keys[8], 71), 0),
    }


CENTER_VALUE = 1.0
HALF_RANGE = 0.8
PENALTY = 1.0
HIGHEST_PRECISION = lax.Precision.HIGHEST


def local_product(stiffness, column_index, vector):
    blocks = vector.shape[0]
    picked = vector[column_index].reshape(blocks, -1, vector.shape[2])
    forward = jnp.einsum("bij,bjr->bir", stiffness, picked, precision=HIGHEST_PRECISION)
    backward = jnp.einsum("bij,bir->bjr", stiffness, vector, precision=HIGHEST_PRECISION)
    backward = backward.reshape(-1, vector.shape[1], vector.shape[2])
    spread = jax.ops.segment_sum(backward, column_index.reshape(-1), num_segments=blocks)
    return forward + spread


def stiffness_apply(operands):
    stiffness, column_index, diagonal, vector = operands
    return diagonal[:, :, None] * vector + local_product(stiffness, column_index, vector)


def chebyshev(operands):
    stiffness, column_index, diagonal, source = operands
    sigma_ratio = CENTER_VALUE / HALF_RANGE
    scale_diag = diagonal[:, :, None]
    residual = source
    solution = jnp.zeros_like(source)
    direction = residual / (CENTER_VALUE * scale_diag)
    ratio_now = 1.0 / sigma_ratio
    for degree in range(DEGREE):
        solution = solution + direction
        if degree + 1 < DEGREE:
            residual = residual - stiffness_apply((stiffness, column_index, diagonal, direction))
            ratio_next = 1.0 / (2.0 * sigma_ratio - ratio_now)
            direction = ratio_next * ratio_now * direction + (2.0 * ratio_next / HALF_RANGE) * residual / scale_diag
            ratio_now = ratio_next
    return solution


def reference(right_side, diagonal, stiffness, column_index, neighbours, face_count, corner_group, coarse_inverse):
    stiff_sub = stiffness.reshape(SUBDOMS, NB, BLOCK, BW * BLOCK)
    column_sub = column_index.reshape(SUBDOMS, NB, BW)
    diag_sub = diagonal.reshape(SUBDOMS, NB, BLOCK)
    device_ids = jnp.arange(SUBDOMS, dtype=jnp.int32)
    partner = (neighbours * N_CORNER + (device_ids % N_CORNER)[:, None]).astype(jnp.int32)
    round_ids = jnp.arange(NNB, dtype=jnp.int32)
    face_mask = (jnp.arange(FMAX, dtype=jnp.int32)[None, None, :] < face_count[:, :, None])[..., None, None]

    def apply_operator(vector):
        local_part = lax.map(stiffness_apply, (stiff_sub, column_sub, diag_sub, vector))
        face_rows = vector[:, :NNB * FMAX].reshape(SUBDOMS, NNB, FMAX, BLOCK, RHS)
        partner_faces = face_rows[partner, round_ids[None, :]]
        coupling = PENALTY * jnp.where(face_mask, face_rows - partner_faces, 0.0)
        return local_part.at[:, :NNB * FMAX].add(coupling.reshape(SUBDOMS, NNB * FMAX, BLOCK, RHS))

    def precondition(vector):
        inner_part = lax.map(chebyshev, (stiff_sub, column_sub, diag_sub, vector))
        corners = vector[:, NB - NCB:].reshape(SUBDOMS * NCB, BLOCK, RHS)
        totals = jax.ops.segment_sum(corners, corner_group.reshape(-1), num_segments=NG).reshape(NCO, RHS)
        coarse = jnp.dot(coarse_inverse, totals, precision=HIGHEST_PRECISION, preferred_element_type=jnp.float32)
        spread = coarse.reshape(NG, BLOCK, RHS)[corner_group]
        return inner_part.at[:, NB - NCB:].add(spread)

    def column_dot(first_vector, second_vector):
        return jnp.sum(first_vector * second_vector, axis=(0, 1, 2))

    residual = right_side.reshape(SUBDOMS, NB, BLOCK, RHS)
    solution = jnp.zeros_like(residual)
    corrected = precondition(residual)
    direction = corrected
    energy_now = column_dot(residual, corrected)
    for iteration in range(ITERS):
        mapped = apply_operator(direction)
        step_size = energy_now / column_dot(direction, mapped)
        solution = solution + step_size * direction
        residual = residual - step_size * mapped
        if iteration + 1 < ITERS:
            corrected = precondition(residual)
            energy_next = column_dot(residual, corrected)
            direction = corrected + (energy_next / energy_now) * direction
            energy_now = energy_next
    return solution.reshape(SUBDOMS * NB, BLOCK, RHS), residual.reshape(SUBDOMS * NB, BLOCK, RHS)
```

```python
import functools

import jax
import jax.numpy as jnp
from jax import lax
from jax.experimental import pallas as pl
from jax.experimental.pallas import tpu as pltpu
from jax.sharding import PartitionSpec as P

F32 = jnp.float32
BF16 = jnp.bfloat16
BLOCK = 64
NB = 16
DOF = NB * BLOCK
RHS = 128
BW = 3
NG = 16
NCB = 8
ROUNDS = 8
DEGREE = 8
HALF_RANGE = 0.8
SIGMA = 1.0 / HALF_RANGE
CHUNK = 128
EXTRA = 8
HEAD = CHUNK + EXTRA
SLOT = HEAD + 2 * BLOCK
TILE = 256
SPLIT = 4
VMEM_LIMIT = 48 * 1024 * 1024


def spec(kind):
    return pl.BlockSpec(memory_space=pltpu.SMEM if kind == "s" else pltpu.VMEM)


def call(body, name, kinds, out_kinds, outs, scratch=(), flops=0):
    return pl.pallas_call(
        body,
        name=name,
        in_specs=[spec(k) for k in kinds],
        out_specs=tuple(spec(k) for k in out_kinds),
        out_shape=tuple(jax.ShapeDtypeStruct(s, t) for s, t in outs),
        scratch_shapes=list(scratch),
        compiler_params=pltpu.CompilerParams(vmem_limit_bytes=VMEM_LIMIT),
        cost_estimate=pl.CostEstimate(
            flops=flops, bytes_accessed=4 * 1024 * 1024, transcendentals=0
        ),
    )


def tiles():
    return [slice(i, i + TILE) for i in range(0, DOF, TILE)]


def put_split(pair, rows, value):
    high = value.astype(BF16)
    pair[rows, :RHS] = high
    pair[rows, RHS:] = (value - high.astype(F32)).astype(BF16)


def product(high, low, pair, rows):
    both = jnp.dot(high[rows, :], pair[...], preferred_element_type=F32)
    rest = jnp.dot(low[rows, :], pair[:, :RHS], preferred_element_type=F32)
    return both[:, :RHS] + (both[:, RHS:] + rest)


def build_kernel(column, stiffness, scale, high, low, inverse, total):
    total[...] = jnp.zeros_like(total)
    lane_half = lax.broadcasted_iota(jnp.int32, (BLOCK, 2 * BLOCK), 1) // BLOCK
    for row in range(NB):
        for link in range(BW):
            part = stiffness[row, :, link * BLOCK : (link + 1) * BLOCK]
            turned = part.T
            target = column[row, link]
            offset = pl.multiple_of((target // 2) * 2 * BLOCK, 2 * BLOCK)
            rows = slice(row * BLOCK, (row + 1) * BLOCK)
            total[rows, pl.ds(offset, 2 * BLOCK)] += jnp.where(
                lane_half == target % 2, jnp.concatenate([part, part], axis=1), 0.0
            )
            lanes = slice((row // 2) * 2 * BLOCK, (row // 2 + 1) * 2 * BLOCK)
            below = pl.ds(pl.multiple_of(target * BLOCK, BLOCK), BLOCK)
            total[below, lanes] += jnp.where(
                lane_half == row % 2, jnp.concatenate([turned, turned], axis=1), 0.0
            )
    for rows in tiles():
        value = total[rows, :]
        top = value.astype(BF16)
        high[rows, :] = top
        low[rows, :] = (value - top.astype(F32)).astype(BF16)
    inverse[...] = 1.0 / scale[...]


def split_kernel(value, high, low):
    for rows in tiles():
        part = value[rows, :]
        top = part.astype(BF16)
        high[rows, :] = top
        low[rows, :] = (part - top.astype(F32)).astype(BF16)


def restrict_into(groups, place, vector, extra, bins, away, keep):
    bins[...] = jnp.zeros_like(bins)
    for corner in range(NCB):
        group = groups[0, corner]
        apart = (group // 2) ^ place[0]
        slot = (apart & 1) * 4 + (apart & 2) + ((apart >> 2) & 1)
        rows = pl.ds(pl.multiple_of((group % 2) * BLOCK, BLOCK), BLOCK)
        first = (NB - NCB + corner) * BLOCK
        bins[slot, rows, :] += vector[first : first + BLOCK, :]
    if extra is not None:
        for slot in range(NCB):
            bins[slot, CHUNK:, :] = extra
    keep[...] = bins[:4]
    away[...] = bins[4:]


def restrict_kernel(groups, place, vector, away, keep, bins):
    restrict_into(groups, place, vector, None, bins, away, keep)


def chebyshev_steps(first, last, scale, inverse, high, low, x, h, e, pairs):
    ratio = 1.0 / SIGMA
    for step in range(last):
        later = 1.0 / (2.0 * SIGMA - ratio)
        if step >= first:
            for rows in tiles():
                now = e[rows, :]
                image = product(high, low, pairs.at[step % 2], rows)
                x[rows, :] = now if step == 0 else x[rows, :] + now
                left = h[rows, :] - (scale[rows, :] * now + image)
                h[rows, :] = left
                new = (later * ratio) * now + (2.0 * later / HALF_RANGE) * (
                    left * inverse[rows, :]
                )
                e[rows, :] = new
                if step + 1 < last:
                    put_split(pairs.at[(step + 1) % 2], rows, new)
        ratio = later


def chebyshev_first(source, scale, inverse, high, low, x, h, e, pairs):
    for rows in tiles():
        value = source[rows, :]
        h[rows, :] = value
        value = value * inverse[rows, :]
        e[rows, :] = value
        put_split(pairs.at[0], rows, value)
    chebyshev_steps(0, SPLIT, scale, inverse, high, low, x, h, e, pairs)


def chebyshev_last(
    with_groups, peers, scale, inverse, high, low, x0, h0, e0, kept, came1, came2, came3, extra,
    y, send, h, e, pairs,
):
    y[...] = x0[...]
    h[...] = h0[...]
    e[...] = e0[...]
    for rows in tiles():
        put_split(pairs.at[SPLIT % 2], rows, e0[rows, :])
    chebyshev_steps(SPLIT, DEGREE - 1, scale, inverse, high, low, y, h, e, pairs)
    y[...] += e[...]
    head = kept[0] + came1[0] + (came2[0] + came3[0])
    for slot in range(NB):
        send[slot, :HEAD, :] = head
        if with_groups:
            send[slot, CHUNK:HEAD, :] = extra[...]
        send[slot, HEAD:, :] = jnp.zeros((2 * BLOCK, RHS), F32)
    for turn in range(ROUNDS):
        send[peers[0, turn], HEAD:, :] = y[turn * 2 * BLOCK : (turn + 1) * 2 * BLOCK, :]


def gather_kernel(received, total, dots):
    value = received[0, :HEAD, :]
    for slot in range(1, NB):
        value = value + received[slot, :HEAD, :]
    total[...] = value[:CHUNK]
    dots[...] = value[CHUNK:]


def column_dot(pairs_of):
    total = None
    for first, second in pairs_of:
        part = jnp.sum(
            (first * second).reshape(first.shape[0] // 8, 8, RHS), axis=0
        )
        total = part if total is None else total + part
    return jnp.sum(total, axis=0, keepdims=True)


def apply_all(
    groups, peers, counts, others, received, y, totals, cih, cil, high, low, scale,
    m, n, coarse, pair,
):
    for rows in tiles():
        put_split(pair, rows, totals[rows, :])
    for rows in tiles():
        coarse[rows, :] = product(cih, cil, pair, rows)

    def block_of(group):
        return coarse[pl.ds(pl.multiple_of(group * BLOCK, BLOCK), BLOCK), :]

    half = (NB - NCB) * BLOCK
    m[:half, :] = y[:half, :]
    for corner in range(NCB):
        rows = slice(half + corner * BLOCK, half + (corner + 1) * BLOCK)
        m[rows, :] = y[rows, :] + block_of(groups[0, corner])
    for rows in tiles():
        put_split(pair, rows, m[rows, :])
    for rows in tiles():
        n[rows, :] = scale[rows, :] * m[rows, :] + product(high, low, pair, rows)
    for block in range(2 * ROUNDS):
        turn, side = block // 2, block % 2
        rows = slice(block * BLOCK, (block + 1) * BLOCK)
        first = HEAD + side * BLOCK
        other = received[peers[0, turn], first : first + BLOCK, :]
        if block >= NB - NCB:
            other = other + block_of(others[0, block - (NB - NCB)])
        n[rows, :] += jnp.where(side < counts[0, turn], m[rows, :] - other, 0.0)


def stage0_kernel(
    groups, place, peers, counts, received, y, totals, cih, cil, high, low, scale, b,
    u, w, away, keep, others, coarse, pair, bins,
):
    lanes = lax.broadcasted_iota(jnp.int32, (1, RHS), 1)
    for corner in range(NCB):
        row = received[peers[0, (NB - NCB + corner) // 2], CHUNK : CHUNK + 1, :]
        picked = jnp.sum(jnp.where(lanes == corner, row, 0.0))
        others[0, corner] = picked.astype(jnp.int32)
    apply_all(
        groups, peers, counts, others, received, y, totals, cih, cil, high, low, scale,
        u, w, coarse, pair,
    )
    energy = column_dot([(b[r, :], u[r, :]) for r in tiles()])
    curve = column_dot([(w[r, :], u[r, :]) for r in tiles()])
    extra = jnp.concatenate([energy, curve, jnp.zeros((EXTRA - 2, RHS), F32)], axis=0)
    restrict_into(groups, place, w, extra, bins, away, keep)


def stage1_kernel(
    groups, place, peers, counts, others, received, y, totals, cih, cil, high, low, scale, b,
    dots, u0, w0,
    m, n, u, w, away, keep, scalars, coarse, pair, bins,
):
    apply_all(
        groups, peers, counts, others, received, y, totals, cih, cil, high, low, scale,
        m, n, coarse, pair,
    )
    energy, curve = dots[0:1, :], dots[1:2, :]
    step = energy / curve
    scalars[...] = jnp.concatenate(
        [energy, curve, step, jnp.zeros((EXTRA - 3, RHS), F32)], axis=0
    )
    for r in tiles():
        u[r, :] = u0[r, :] - step * m[r, :]
        w[r, :] = w0[r, :] - step * n[r, :]
    new_energy = column_dot([(b[r, :] - step * w0[r, :], u[r, :]) for r in tiles()])
    new_curve = column_dot([(w[r, :], u[r, :]) for r in tiles()])
    cross = column_dot(
        [(u[r, :], w0[r, :]) for r in tiles()] + [(u0[r, :], w[r, :]) for r in tiles()]
    )
    extra = jnp.concatenate(
        [new_energy, new_curve, cross, jnp.zeros((EXTRA - 3, RHS), F32)], axis=0
    )
    restrict_into(groups, place, w, extra, bins, away, keep)


def stage2_kernel(
    groups, peers, counts, others, received, y, totals, cih, cil, high, low, scale, b,
    dots, before, u0, w0, m0, n0, u1, w1,
    p, s, u, w, last, scalars, m, n, coarse, pair,
):
    apply_all(
        groups, peers, counts, others, received, y, totals, cih, cil, high, low, scale,
        m, n, coarse, pair,
    )
    energy0, curve0, step0 = before[0:1, :], before[1:2, :], before[2:3, :]
    energy, delta, cross = dots[0:1, :], dots[1:2, :], dots[2:3, :]
    beta = energy / energy0
    curve = delta + beta * cross + beta * beta * curve0
    step = energy / curve
    scalars[...] = jnp.concatenate(
        [energy, curve, step, step0, jnp.zeros((EXTRA - 4, RHS), F32)], axis=0
    )
    for r in tiles():
        p[r, :] = u1[r, :] + beta * u0[r, :]
        s[r, :] = w1[r, :] + beta * w0[r, :]
        u[r, :] = u1[r, :] - step * (m[r, :] + beta * m0[r, :])
        w[r, :] = w1[r, :] - step * (n[r, :] + beta * n0[r, :])
    new_energy = column_dot(
        [((b[r, :] - step0 * w0[r, :]) - step * s[r, :], u[r, :]) for r in tiles()]
    )
    new_curve = column_dot([(w[r, :], u[r, :]) for r in tiles()])
    cross = column_dot(
        [(u[r, :], s[r, :]) for r in tiles()] + [(p[r, :], w[r, :]) for r in tiles()]
    )
    for slot in range(last.shape[0]):
        last[slot, 0:1, :] = new_energy
        last[slot, 1:2, :] = new_curve
        last[slot, 2:3, :] = cross


def finish_kernel(all_dots, scalars, b, u0, w0, p, s, u, w, solution, residual):
    value = jnp.sum(all_dots[...], axis=0)
    energy, delta, cross = value[0:1, :], value[1:2, :], value[2:3, :]
    before, curve0 = scalars[0:1, :], scalars[1:2, :]
    step1, step0 = scalars[2:3, :], scalars[3:4, :]
    beta = energy / before
    step = energy / (delta + beta * cross + beta * beta * curve0)
    along = step1 + step * beta
    for r in tiles():
        solution[r, :] = step0 * u0[r, :] + along * p[r, :] + step * u[r, :]
        residual[r, :] = (
            (b[r, :] - step0 * w0[r, :]) - along * s[r, :] - step * w[r, :]
        )


FIELD = ((DOF, RHS), F32)
MATRIX = ((DOF, DOF), BF16)
HALF_BINS = ((4, HEAD, RHS), F32)
SMALL = ((EXTRA, RHS), F32)
PAIR = pltpu.VMEM((DOF, 2 * RHS), BF16)
PAIRS = pltpu.VMEM((2, DOF, 2 * RHS), BF16)
FIELD_SCRATCH = pltpu.VMEM((DOF, RHS), F32)
BINS = pltpu.VMEM((NCB, HEAD, RHS), F32)
STEP_FLOPS = 2 * DOF * DOF * RHS * 3


def on_device(
    right_side,
    diagonal,
    stiffness,
    column_index,
    neighbours,
    face_count,
    corner_group,
    coarse_inverse,
):
    corners = lax.axis_size("corner")
    devices = corners * lax.axis_size("sub")
    b = right_side.reshape(DOF, RHS)
    place = lax.axis_index("corner").astype(jnp.int32).reshape(1)
    whole_inverse = lax.all_gather(coarse_inverse, "corner", axis=0, tiled=True)
    group_row = jnp.zeros((EXTRA, RHS), F32).at[0, :NCB].set(corner_group[0].astype(F32))
    scale = jnp.broadcast_to(diagonal.reshape(DOF, 1), (DOF, RHS))

    def exchange(array, bit):
        return lax.ppermute(array, "corner", [(i, i ^ bit) for i in range(corners)])

    def precondition(source, away, keep, extra):
        came1 = exchange(away, 1)
        x, h, e = call(
            chebyshev_first, "chebyshev_first", "vvvvv", "vvv", [FIELD] * 3, [PAIRS],
            STEP_FLOPS * SPLIT,
        )(source, scale, inverse, high, low)
        came2 = exchange(keep[2:] + came1[2:], 2)
        came3 = exchange(keep[1:2] + came1[1:2] + came2[1:2], 4)
        y, send = call(
            functools.partial(chebyshev_last, extra is not None), "chebyshev_last",
            "svvvvvvvvvvvv", "vv", [FIELD, ((NB, SLOT, RHS), F32)],
            [FIELD_SCRATCH, FIELD_SCRATCH, PAIRS], STEP_FLOPS * (DEGREE - 1 - SPLIT),
        )(
            neighbours, scale, inverse, high, low, x, h, e, keep, came1, came2, came3,
            group_row,
        )
        received = lax.all_to_all(send, "sub", 0, 0, tiled=True)
        total, dots = call(
            gather_kernel, "gather", "v", "vv", [((CHUNK, RHS), F32), SMALL]
        )(received)
        totals = lax.all_gather(total, "corner", axis=0, tiled=True)
        return received, y, totals, dots

    away, keep = call(
        restrict_kernel, "restrict", "ssv", "vv", [HALF_BINS] * 2, [BINS]
    )(corner_group, place, b)
    high, low, inverse = call(
        build_kernel, "build", "svv", "vvv", [MATRIX, MATRIX, FIELD],
        [pltpu.VMEM((DOF, DOF), F32)], STEP_FLOPS * 3,
    )(column_index, stiffness, scale)
    cih, cil = call(split_kernel, "split", "v", "vv", [MATRIX, MATRIX])(whole_inverse)

    received, y, totals, _ = precondition(b, away, keep, group_row)
    u0, w0, away, keep, others = call(
        stage0_kernel, "stage0", "ssssvvvvvvvvv", "vvvvs",
        [FIELD, FIELD, HALF_BINS, HALF_BINS, ((1, NCB), jnp.int32)],
        [FIELD_SCRATCH, PAIR, BINS], STEP_FLOPS * 2,
    )(
        corner_group, place, neighbours, face_count, received, y, totals, cih, cil,
        high, low, scale, b,
    )
    received, y, totals, dots = precondition(w0, away, keep, None)
    m0, n0, u1, w1, away, keep, before = call(
        stage1_kernel, "stage1", "sssssvvvvvvvvvvvv", "vvvvvvv",
        [FIELD] * 4 + [HALF_BINS, HALF_BINS, SMALL],
        [FIELD_SCRATCH, PAIR, BINS], STEP_FLOPS * 2,
    )(
        corner_group, place, neighbours, face_count, others, received, y, totals, cih, cil,
        high, low, scale, b, dots, u0, w0,
    )
    received, y, totals, dots = precondition(w1, away, keep, None)
    p, s, u2, w2, last, scalars = call(
        stage2_kernel, "stage2", "ssssvvvvvvvvvvvvvvvvv", "vvvvvv",
        [FIELD] * 4 + [((devices, 3, RHS), F32), SMALL],
        [FIELD_SCRATCH, FIELD_SCRATCH, FIELD_SCRATCH, PAIR], STEP_FLOPS * 2,
    )(
        corner_group, neighbours, face_count, others, received, y, totals, cih, cil,
        high, low, scale, b, dots, before, u0, w0, m0, n0, u1, w1,
    )
    all_dots = lax.all_to_all(last, ("sub", "corner"), 0, 0, tiled=True)
    solution, residual = call(
        finish_kernel, "finish", "vvvvvvvvv", "vv", [FIELD, FIELD]
    )(all_dots, scalars, b, u0, w0, p, s, u2, w2)
    return (solution.reshape(right_side.shape), residual.reshape(right_side.shape))


def solution(mesh):
    placed = (
        P(("sub", "corner"), None, None),
        P(("sub", "corner"), None),
        P(("sub", "corner"), None, None),
        P(("sub", "corner"), None),
        P(("sub", "corner"), None),
        P(("sub", "corner"), None),
        P(("sub", "corner"), None),
        P("corner", None),
    )
    return jax.shard_map(
        on_device,
        mesh=mesh,
        in_specs=placed,
        out_specs=(P(("sub", "corner"), None, None), P(("sub", "corner"), None, None)),
        check_vma=False,
    )
```

```python
import functools
import math

import jax
import jax.numpy as jnp
from jax import lax
from jax.experimental import pallas as pl
from jax.experimental.pallas import tpu as pltpu
from jax.sharding import PartitionSpec as P

F32 = jnp.float32
BF16 = jnp.bfloat16
BLOCK = 64
NB = 16
DOF = NB * BLOCK
RHS = 128
BW = 3
NG = 16
NCB = 8
ROUNDS = 8
DEGREE = 8
HALF_RANGE = 0.8
SIGMA = 1.0 / HALF_RANGE
CHUNK = 128
PIECE = 8
EXTRA = 8
HEAD = PIECE + EXTRA
SLOT = HEAD + 2 * BLOCK
TILE = 256
CUTS = (0, 1, 6)
VMEM_ROOM = 3 * 1024 * 1024


def spec(kind):
    return pl.BlockSpec(memory_space=pltpu.SMEM if kind == "s" else pltpu.VMEM)


def nbytes(shape, dtype):
    lanes = -(-shape[-1] // 128) * 128
    rows = -(-shape[-2] // 8) * 8
    return math.prod(shape[:-2]) * rows * lanes * jnp.dtype(dtype).itemsize


def call(body, name, kinds, out_kinds, outs, scratch=(), flops=0):
    def run(*operands):
        vmem = [(a.shape, a.dtype) for a, k in zip(operands, kinds, strict=True) if k == "v"]
        vmem += [o for o, k in zip(outs, out_kinds, strict=True) if k == "v"]
        vmem += [(s.shape, s.dtype) for s in scratch]
        return pl.pallas_call(
            body,
            name=name,
            in_specs=[spec(k) for k in kinds],
            out_specs=tuple(spec(k) for k in out_kinds),
            out_shape=tuple(jax.ShapeDtypeStruct(s, t) for s, t in outs),
            scratch_shapes=list(scratch),
            compiler_params=pltpu.CompilerParams(
                vmem_limit_bytes=VMEM_ROOM + sum(nbytes(*v) for v in vmem)
            ),
            cost_estimate=pl.CostEstimate(
                flops=flops, bytes_accessed=4 * 1024 * 1024, transcendentals=0
            ),
        )(*operands)

    return run


def tiles():
    return [slice(i, i + TILE) for i in range(0, DOF, TILE)]


def put_split(pair, rows, value):
    high = value.astype(BF16)
    pair[rows, :RHS] = high
    pair[rows, RHS:] = (value - high.astype(F32)).astype(BF16)


def product(high, low, pair, rows):
    both = jnp.dot(high[rows, :], pair[...], preferred_element_type=F32)
    rest = jnp.dot(low[rows, :], pair[:, :RHS], preferred_element_type=F32)
    return both[:, :RHS] + (both[:, RHS:] + rest)


def build_kernel(
    column, groups, place, stiffness, scale, b,
    high, low, inverse, away, keep, turned, even, odd, source, bins,
):
    restrict_into(groups, place, b, None, bins, away, keep)
    lane_half = lax.broadcasted_iota(jnp.int32, (BLOCK, 2 * BLOCK), 1) // BLOCK
    for pair in range(NB // 2):
        tile = stiffness[2 * pair : 2 * pair + 2]
        first = tile[:, :, : 2 * BLOCK].reshape(2 * BLOCK, 2 * BLOCK).T
        turned[pair, 0] = first[:BLOCK]
        turned[pair, 1] = first[BLOCK:]
        turned[pair, 2] = tile[:, :, 2 * BLOCK :].reshape(2 * BLOCK, BLOCK).T
    for row in range(NB):
        for link in range(BW):
            source[column[row, link], link] = row
    for row in range(NB):
        panel = odd if row % 2 else even
        panel[...] = jnp.zeros_like(panel)
        tile = stiffness[row, :, : 2 * BLOCK]
        swapped = pltpu.roll(tile, BLOCK, 1)
        last = stiffness[row, :, 2 * BLOCK :]
        twice = (
            jnp.where(lane_half == 0, tile, swapped),
            jnp.where(lane_half == 1, tile, swapped),
            jnp.concatenate([last, last], axis=1),
        )
        for link in range(BW):
            origin = source[row, link]
            for column_block, block in (
                (column[row, link], twice[link]),
                (origin, turned[origin // 2, link]),
            ):
                lanes = pl.ds(
                    pl.multiple_of((column_block // 2) * 2 * BLOCK, 2 * BLOCK), 2 * BLOCK
                )
                panel[:, lanes] += jnp.where(lane_half == column_block % 2, block, 0.0)
        rows = slice(row * BLOCK, (row + 1) * BLOCK)
        value = panel[...]
        top = value.astype(BF16)
        high[rows, :] = top
        low[rows, :] = (value - top.astype(F32)).astype(BF16)
    inverse[...] = 1.0 / scale[...]


def split_kernel(value, high, low):
    for rows in tiles():
        part = value[rows, :]
        top = part.astype(BF16)
        high[rows, :] = top
        low[rows, :] = (part - top.astype(F32)).astype(BF16)


def restrict_into(groups, place, vector, extra, bins, away, keep):
    bins[...] = jnp.zeros_like(bins)
    for corner in range(NCB):
        group = groups[0, corner]
        apart = (group // 2) ^ place[0]
        slot = (apart & 1) * 4 + (apart & 2) + ((apart >> 2) & 1)
        rows = pl.ds(pl.multiple_of((group % 2) * BLOCK, BLOCK), BLOCK)
        first = (NB - NCB + corner) * BLOCK
        bins[slot, rows, :] += vector[first : first + BLOCK, :]
    if extra is not None:
        for slot in range(NCB):
            bins[slot, CHUNK:, :] = extra
    keep[...] = bins[:4]
    away[...] = bins[4:]


def chebyshev_steps(first, last, scale, inverse, high, low, x, h, e, pairs):
    ratio = 1.0 / SIGMA
    for step in range(last):
        later = 1.0 / (2.0 * SIGMA - ratio)
        if step >= first:
            for rows in tiles():
                now = e[rows, :]
                image = product(high, low, pairs.at[step % 2], rows)
                x[rows, :] = now if step == 0 else x[rows, :] + now
                left = h[rows, :] - (scale[rows, :] * now + image)
                h[rows, :] = left
                new = (later * ratio) * now + (2.0 * later / HALF_RANGE) * (
                    left * inverse[rows, :]
                )
                e[rows, :] = new
                if step + 1 < last:
                    put_split(pairs.at[(step + 1) % 2], rows, new)
        ratio = later


def chebyshev_first(last, source, scale, inverse, high, low, x, h, e, pairs):
    for rows in tiles():
        value = source[rows, :]
        h[rows, :] = value
        value = value * inverse[rows, :]
        e[rows, :] = value
        put_split(pairs.at[0], rows, value)
    chebyshev_steps(0, last, scale, inverse, high, low, x, h, e, pairs)


def resume(first, x0, h0, e0, x, h, e, pairs):
    for rows in tiles():
        x[rows, :] = x0[rows, :]
        h[rows, :] = h0[rows, :]
        value = e0[rows, :]
        e[rows, :] = value
        put_split(pairs.at[first % 2], rows, value)


def chebyshev_middle(first, last, x0, h0, e0, scale, inverse, high, low, x, h, e, pairs):
    resume(first, x0, h0, e0, x, h, e, pairs)
    chebyshev_steps(first, last, scale, inverse, high, low, x, h, e, pairs)


def chebyshev_last(
    with_groups, first, peers, groups, scale, inverse, high, low, x0, h0, e0, kept, came1,
    came2, came3, came4, y, send, h, e, pairs,
):
    resume(first, x0, h0, e0, y, h, e, pairs)
    chebyshev_steps(first, DEGREE - 1, scale, inverse, high, low, y, h, e, pairs)
    y[...] += e[...]
    head = kept[0] + came1[0] + (came2[0] + came3[0] + came4[0])
    tail = head[CHUNK:, :]
    if with_groups:
        lanes = lax.broadcasted_iota(jnp.int32, (EXTRA, RHS), 1)
        tail = jnp.zeros((EXTRA, RHS), F32)
        for corner in range(NCB):
            group = groups[0, corner].astype(F32)
            tail = jnp.where(lanes == corner, group, tail)
    for slot in range(NB):
        send[slot, :PIECE, :] = head[slot * PIECE : (slot + 1) * PIECE, :]
        send[slot, PIECE:HEAD, :] = tail
        send[slot, HEAD:, :] = jnp.zeros((2 * BLOCK, RHS), F32)
    for turn in range(ROUNDS):
        send[peers[0, turn], HEAD:, :] = y[turn * 2 * BLOCK : (turn + 1) * 2 * BLOCK, :]


def gather_kernel(received, pieces, dots):
    value = received[0, :HEAD, :]
    for slot in range(1, NB):
        value = value + received[slot, :HEAD, :]
    for device in range(pieces.shape[0]):
        pieces[device] = value[:PIECE]
    dots[...] = value[PIECE:]


def column_dot(pairs_of):
    total = None
    for first, second in pairs_of:
        part = jnp.sum(
            (first * second).reshape(first.shape[0] // 8, 8, RHS), axis=0
        )
        total = part if total is None else total + part
    return jnp.sum(total, axis=0, keepdims=True)


def apply_all(
    groups, peers, counts, others, received, y, totals, cih, cil, high, low, scale,
    m, n, coarse, pair,
):
    for device in range(totals.shape[0]):
        first = (device % NCB) * CHUNK + (device // NCB) * PIECE
        coarse[first : first + PIECE, :] = totals[device]
    for rows in tiles():
        put_split(pair, rows, coarse[rows, :])
    for rows in tiles():
        coarse[rows, :] = product(cih, cil, pair, rows)

    def block_of(group):
        return coarse[pl.ds(pl.multiple_of(group * BLOCK, BLOCK), BLOCK), :]

    half = (NB - NCB) * BLOCK
    m[:half, :] = y[:half, :]
    for corner in range(NCB):
        rows = slice(half + corner * BLOCK, half + (corner + 1) * BLOCK)
        m[rows, :] = y[rows, :] + block_of(groups[0, corner])
    for rows in tiles():
        put_split(pair, rows, m[rows, :])
    for rows in tiles():
        n[rows, :] = scale[rows, :] * m[rows, :] + product(high, low, pair, rows)
    for block in range(2 * ROUNDS):
        turn, side = block // 2, block % 2
        rows = slice(block * BLOCK, (block + 1) * BLOCK)
        first = HEAD + side * BLOCK
        other = received[peers[0, turn], first : first + BLOCK, :]
        if block >= NB - NCB:
            other = other + block_of(others[0, block - (NB - NCB)])
        n[rows, :] += jnp.where(side < counts[0, turn], m[rows, :] - other, 0.0)


def stage0_kernel(
    groups, place, peers, counts, received, y, totals, cih, cil, high, low, scale, b,
    u, w, away, keep, others, coarse, pair, bins,
):
    lanes = lax.broadcasted_iota(jnp.int32, (1, RHS), 1)
    for corner in range(NCB):
        row = received[peers[0, (NB - NCB + corner) // 2], PIECE : PIECE + 1, :]
        picked = jnp.sum(jnp.where(lanes == corner, row, 0.0))
        others[0, corner] = picked.astype(jnp.int32)
    apply_all(
        groups, peers, counts, others, received, y, totals, cih, cil, high, low, scale,
        u, w, coarse, pair,
    )
    energy = column_dot([(b[r, :], u[r, :]) for r in tiles()])
    curve = column_dot([(w[r, :], u[r, :]) for r in tiles()])
    extra = jnp.concatenate([energy, curve, jnp.zeros((EXTRA - 2, RHS), F32)], axis=0)
    restrict_into(groups, place, w, extra, bins, away, keep)


def stage1_kernel(
    groups, place, peers, counts, others, received, y, totals, cih, cil, high, low, scale, b,
    dots, u0, w0,
    m, n, u, w, away, keep, scalars, coarse, pair, bins,
):
    apply_all(
        groups, peers, counts, others, received, y, totals, cih, cil, high, low, scale,
        m, n, coarse, pair,
    )
    energy, curve = dots[0:1, :], dots[1:2, :]
    step = energy / curve
    scalars[...] = jnp.concatenate(
        [energy, curve, step, jnp.zeros((EXTRA - 3, RHS), F32)], axis=0
    )
    for r in tiles():
        u[r, :] = u0[r, :] - step * m[r, :]
        w[r, :] = w0[r, :] - step * n[r, :]
    new_energy = column_dot([(b[r, :] - step * w0[r, :], u[r, :]) for r in tiles()])
    new_curve = column_dot([(w[r, :], u[r, :]) for r in tiles()])
    cross = column_dot(
        [(u[r, :], w0[r, :]) for r in tiles()] + [(u0[r, :], w[r, :]) for r in tiles()]
    )
    extra = jnp.concatenate(
        [new_energy, new_curve, cross, jnp.zeros((EXTRA - 3, RHS), F32)], axis=0
    )
    restrict_into(groups, place, w, extra, bins, away, keep)


def stage2_kernel(
    groups, peers, counts, others, received, y, totals, cih, cil, high, low, scale, b,
    dots, before, u0, w0, m0, n0, u1, w1,
    p, s, u, w, last, scalars, m, n, coarse, pair,
):
    apply_all(
        groups, peers, counts, others, received, y, totals, cih, cil, high, low, scale,
        m, n, coarse, pair,
    )
    energy0, curve0, step0 = before[0:1, :], before[1:2, :], before[2:3, :]
    energy, delta, cross = dots[0:1, :], dots[1:2, :], dots[2:3, :]
    beta = energy / energy0
    curve = delta + beta * cross + beta * beta * curve0
    step = energy / curve
    scalars[...] = jnp.concatenate(
        [energy, curve, step, step0, jnp.zeros((EXTRA - 4, RHS), F32)], axis=0
    )
    for r in tiles():
        p[r, :] = u1[r, :] + beta * u0[r, :]
        s[r, :] = w1[r, :] + beta * w0[r, :]
        u[r, :] = u1[r, :] - step * (m[r, :] + beta * m0[r, :])
        w[r, :] = w1[r, :] - step * (n[r, :] + beta * n0[r, :])
    new_energy = column_dot(
        [((b[r, :] - step0 * w0[r, :]) - step * s[r, :], u[r, :]) for r in tiles()]
    )
    new_curve = column_dot([(w[r, :], u[r, :]) for r in tiles()])
    cross = column_dot(
        [(u[r, :], s[r, :]) for r in tiles()] + [(p[r, :], w[r, :]) for r in tiles()]
    )
    for slot in range(last.shape[0]):
        last[slot, 0:1, :] = new_energy
        last[slot, 1:2, :] = new_curve
        last[slot, 2:3, :] = cross


def finish_kernel(all_dots, scalars, b, u0, w0, p, s, u, w, solution, residual):
    value = jnp.sum(all_dots[...], axis=0)
    energy, delta, cross = value[0:1, :], value[1:2, :], value[2:3, :]
    before, curve0 = scalars[0:1, :], scalars[1:2, :]
    step1, step0 = scalars[2:3, :], scalars[3:4, :]
    beta = energy / before
    step = energy / (delta + beta * cross + beta * beta * curve0)
    along = step1 + step * beta
    for r in tiles():
        solution[r, :] = step0 * u0[r, :] + along * p[r, :] + step * u[r, :]
        residual[r, :] = (
            (b[r, :] - step0 * w0[r, :]) - along * s[r, :] - step * w[r, :]
        )


FIELD = ((DOF, RHS), F32)
MATRIX = ((DOF, DOF), BF16)
HALF_BINS = ((4, CHUNK + EXTRA, RHS), F32)
SMALL = ((EXTRA, RHS), F32)
PAIR = pltpu.VMEM((DOF, 2 * RHS), BF16)
PAIRS = pltpu.VMEM((2, DOF, 2 * RHS), BF16)
FIELD_SCRATCH = pltpu.VMEM((DOF, RHS), F32)
BINS = pltpu.VMEM((NCB, CHUNK + EXTRA, RHS), F32)
STEP_FLOPS = 2 * DOF * DOF * RHS * 3


def on_device(
    right_side,
    diagonal,
    stiffness,
    column_index,
    neighbours,
    face_count,
    corner_group,
    coarse_inverse,
):
    corners = lax.axis_size("corner")
    devices = corners * lax.axis_size("sub")
    b = right_side.reshape(DOF, RHS)
    place = lax.axis_index("corner").astype(jnp.int32).reshape(1)
    whole_inverse = lax.all_gather(coarse_inverse, "corner", axis=0, tiled=True)
    scale = jnp.broadcast_to(diagonal.reshape(DOF, 1), (DOF, RHS))

    def exchange(array, bit):
        return lax.ppermute(array, "corner", [(i, i ^ bit) for i in range(corners)])

    def middle(first, last, state):
        return call(
            functools.partial(chebyshev_middle, first, last), f"chebyshev_{first}", "vvvvvvv",
            "vvv", [FIELD] * 3, [PAIRS], STEP_FLOPS * (last - first),
        )(*state, scale, inverse, high, low)

    def precondition(source, away, keep, with_groups):
        came1 = exchange(away, 1)
        state = call(
            functools.partial(chebyshev_first, CUTS[1]), "chebyshev_first", "vvvvv", "vvv",
            [FIELD] * 3, [PAIRS], STEP_FLOPS * CUTS[1],
        )(source, scale, inverse, high, low)
        rest = keep[1:] + came1[1:]
        rest, *state = lax.optimization_barrier((rest, *state))
        came2 = exchange(rest[1:2], 2)
        came3 = exchange(rest[0:1], 4)
        came4 = exchange(rest[2:3], 6)
        state = middle(CUTS[1], CUTS[2], state)
        y, send = call(
            functools.partial(chebyshev_last, with_groups, CUTS[2]), "chebyshev_last",
            "ssvvvvvvvvvvvv", "vv", [FIELD, ((NB, SLOT, RHS), F32)],
            [FIELD_SCRATCH, FIELD_SCRATCH, PAIRS], STEP_FLOPS * (DEGREE - 1 - CUTS[2]),
        )(
            neighbours, corner_group, scale, inverse, high, low, *state, keep, came1,
            came2, came3, came4,
        )
        received = lax.all_to_all(send, "sub", 0, 0, tiled=True)
        pieces, dots = call(
            gather_kernel, "gather", "v", "vv", [((devices, PIECE, RHS), F32), SMALL]
        )(received)
        if with_groups:
            pieces, *_ = lax.optimization_barrier((pieces, cih, cil))
        totals = lax.all_to_all(pieces, ("sub", "corner"), 0, 0, tiled=True)
        return received, y, totals, dots

    high, low, inverse, away, keep = call(
        build_kernel, "build", "sssvvv", "vvvvv",
        [MATRIX, MATRIX, FIELD, HALF_BINS, HALF_BINS],
        [
            pltpu.VMEM((NB // 2, BW, BLOCK, 2 * BLOCK), F32),
            pltpu.VMEM((BLOCK, DOF), F32),
            pltpu.VMEM((BLOCK, DOF), F32),
            pltpu.SMEM((NB, BW), jnp.int32),
            BINS,
        ],
        STEP_FLOPS * 3,
    )(column_index, corner_group, place, stiffness, scale, b)
    cih, cil = call(split_kernel, "split", "v", "vv", [MATRIX, MATRIX])(whole_inverse)

    received, y, totals, _ = precondition(b, away, keep, True)
    u0, w0, away, keep, others = call(
        stage0_kernel, "stage0", "ssssvvvvvvvvv", "vvvvs",
        [FIELD, FIELD, HALF_BINS, HALF_BINS, ((1, NCB), jnp.int32)],
        [FIELD_SCRATCH, PAIR, BINS], STEP_FLOPS * 2,
    )(
        corner_group, place, neighbours, face_count, received, y, totals, cih, cil,
        high, low, scale, b,
    )
    received, y, totals, dots = precondition(w0, away, keep, False)
    m0, n0, u1, w1, away, keep, before = call(
        stage1_kernel, "stage1", "sssssvvvvvvvvvvvv", "vvvvvvv",
        [FIELD] * 4 + [HALF_BINS, HALF_BINS, SMALL],
        [FIELD_SCRATCH, PAIR, BINS], STEP_FLOPS * 2,
    )(
        corner_group, place, neighbours, face_count, others, received, y, totals, cih, cil,
        high, low, scale, b, dots, u0, w0,
    )
    received, y, totals, dots = precondition(w1, away, keep, False)
    p, s, u2, w2, last, scalars = call(
        stage2_kernel, "stage2", "ssssvvvvvvvvvvvvvvvvv", "vvvvvv",
        [FIELD] * 4 + [((devices, 3, RHS), F32), SMALL],
        [FIELD_SCRATCH, FIELD_SCRATCH, FIELD_SCRATCH, PAIR], STEP_FLOPS * 2,
    )(
        corner_group, neighbours, face_count, others, received, y, totals, cih, cil,
        high, low, scale, b, dots, before, u0, w0, m0, n0, u1, w1,
    )
    all_dots = lax.all_to_all(last, ("sub", "corner"), 0, 0, tiled=True)
    solution, residual = call(
        finish_kernel, "finish", "vvvvvvvvv", "vv", [FIELD, FIELD]
    )(all_dots, scalars, b, u0, w0, p, s, u2, w2)
    return (solution.reshape(right_side.shape), residual.reshape(right_side.shape))


def solution(mesh):
    placed = (
        P(("sub", "corner"), None, None),
        P(("sub", "corner"), None),
        P(("sub", "corner"), None, None),
        P(("sub", "corner"), None),
        P(("sub", "corner"), None),
        P(("sub", "corner"), None),
        P(("sub", "corner"), None),
        P("corner", None),
    )
    return jax.shard_map(
        on_device,
        mesh=mesh,
        in_specs=placed,
        out_specs=(P(("sub", "corner"), None, None), P(("sub", "corner"), None, None)),
        check_vma=False,
    )
```

```python
import functools
import math

import jax
import jax.numpy as jnp
from jax import lax
from jax.experimental import pallas as pl
from jax.experimental.pallas import tpu as pltpu
from jax.sharding import PartitionSpec as P

F32 = jnp.float32
BF16 = jnp.bfloat16
BLOCK = 64
NB = 16
DOF = NB * BLOCK
RHS = 128
BW = 3
NG = 16
NCB = 8
ROUNDS = 8
DEGREE = 8
HALF_RANGE = 0.8
SIGMA = 1.0 / HALF_RANGE
CHUNK = 128
PIECE = CHUNK // 2
EXTRA = 8
HEAD = PIECE + EXTRA
SLOT = HEAD + 2 * BLOCK
TILE = 256
CUTS = (0, 1, 4, 6)
VMEM_ROOM = 3 * 1024 * 1024


def spec(kind):
    return pl.BlockSpec(memory_space=pltpu.SMEM if kind == "s" else pltpu.VMEM)


def nbytes(shape, dtype):
    lanes = -(-shape[-1] // 128) * 128
    rows = -(-shape[-2] // 8) * 8
    return math.prod(shape[:-2]) * rows * lanes * jnp.dtype(dtype).itemsize


def call(body, name, kinds, out_kinds, outs, scratch=(), flops=0):
    def run(*operands):
        vmem = [(a.shape, a.dtype) for a, k in zip(operands, kinds, strict=True) if k == "v"]
        vmem += [o for o, k in zip(outs, out_kinds, strict=True) if k == "v"]
        vmem += [(s.shape, s.dtype) for s in scratch]
        return pl.pallas_call(
            body,
            name=name,
            in_specs=[spec(k) for k in kinds],
            out_specs=tuple(spec(k) for k in out_kinds),
            out_shape=tuple(jax.ShapeDtypeStruct(s, t) for s, t in outs),
            scratch_shapes=list(scratch),
            compiler_params=pltpu.CompilerParams(
                vmem_limit_bytes=VMEM_ROOM + sum(nbytes(*v) for v in vmem)
            ),
            cost_estimate=pl.CostEstimate(
                flops=flops, bytes_accessed=4 * 1024 * 1024, transcendentals=0
            ),
        )(*operands)

    return run


def tiles():
    return [slice(i, i + TILE) for i in range(0, DOF, TILE)]


def put_split(pair, rows, value):
    high = value.astype(BF16)
    pair[rows, :RHS] = high
    pair[rows, RHS:] = (value - high.astype(F32)).astype(BF16)


def product(high, low, pair, rows):
    both = jnp.dot(high[rows, :], pair[...], preferred_element_type=F32)
    rest = jnp.dot(low[rows, :], pair[:, :RHS], preferred_element_type=F32)
    return both[:, :RHS] + (both[:, RHS:] + rest)


def build_kernel(
    column, groups, place, stiffness, scale, b,
    high, low, inverse, away, keep, turned, even, odd, source, bins,
):
    restrict_into(groups, place, b, None, bins, away, keep)
    lane_half = lax.broadcasted_iota(jnp.int32, (BLOCK, 2 * BLOCK), 1) // BLOCK
    for pair in range(NB // 2):
        tile = stiffness[2 * pair : 2 * pair + 2]
        first = tile[:, :, : 2 * BLOCK].reshape(2 * BLOCK, 2 * BLOCK).T
        turned[pair, 0] = first[:BLOCK]
        turned[pair, 1] = first[BLOCK:]
        turned[pair, 2] = tile[:, :, 2 * BLOCK :].reshape(2 * BLOCK, BLOCK).T
    for row in range(NB):
        for link in range(BW):
            source[column[row, link], link] = row
    for row in range(NB):
        panel = odd if row % 2 else even
        panel[...] = jnp.zeros_like(panel)
        tile = stiffness[row, :, : 2 * BLOCK]
        swapped = pltpu.roll(tile, BLOCK, 1)
        last = stiffness[row, :, 2 * BLOCK :]
        twice = (
            jnp.where(lane_half == 0, tile, swapped),
            jnp.where(lane_half == 1, tile, swapped),
            jnp.concatenate([last, last], axis=1),
        )
        for link in range(BW):
            origin = source[row, link]
            for column_block, block in (
                (column[row, link], twice[link]),
                (origin, turned[origin // 2, link]),
            ):
                lanes = pl.ds(
                    pl.multiple_of((column_block // 2) * 2 * BLOCK, 2 * BLOCK), 2 * BLOCK
                )
                panel[:, lanes] += jnp.where(lane_half == column_block % 2, block, 0.0)
        rows = slice(row * BLOCK, (row + 1) * BLOCK)
        value = panel[...]
        top = value.astype(BF16)
        high[rows, :] = top
        low[rows, :] = (value - top.astype(F32)).astype(BF16)
    inverse[...] = 1.0 / scale[...]


def split_kernel(value, high, low):
    for rows in tiles():
        part = value[rows, :]
        top = part.astype(BF16)
        high[rows, :] = top
        low[rows, :] = (part - top.astype(F32)).astype(BF16)


def restrict_into(groups, place, vector, extra, bins, away, keep):
    bins[...] = jnp.zeros_like(bins)
    for corner in range(NCB):
        group = groups[0, corner]
        apart = (group // 2) ^ place[0]
        slot = (apart & 1) * 4 + (apart & 2) + ((apart >> 2) & 1)
        rows = pl.ds(pl.multiple_of((group % 2) * BLOCK, BLOCK), BLOCK)
        first = (NB - NCB + corner) * BLOCK
        bins[slot, rows, :] += vector[first : first + BLOCK, :]
    if extra is not None:
        for slot in range(NCB):
            bins[slot, CHUNK:, :] = extra
    keep[...] = bins[:4]
    away[...] = bins[4:]


def chebyshev_steps(first, last, scale, inverse, high, low, x, h, e, pairs):
    ratio = 1.0 / SIGMA
    for step in range(last):
        later = 1.0 / (2.0 * SIGMA - ratio)
        if step >= first:
            for rows in tiles():
                now = e[rows, :]
                image = product(high, low, pairs.at[step % 2], rows)
                x[rows, :] = now if step == 0 else x[rows, :] + now
                left = h[rows, :] - (scale[rows, :] * now + image)
                h[rows, :] = left
                new = (later * ratio) * now + (2.0 * later / HALF_RANGE) * (
                    left * inverse[rows, :]
                )
                e[rows, :] = new
                if step + 1 < last:
                    put_split(pairs.at[(step + 1) % 2], rows, new)
        ratio = later


def chebyshev_first(last, source, scale, inverse, high, low, x, h, e, pairs):
    for rows in tiles():
        value = source[rows, :]
        h[rows, :] = value
        value = value * inverse[rows, :]
        e[rows, :] = value
        put_split(pairs.at[0], rows, value)
    chebyshev_steps(0, last, scale, inverse, high, low, x, h, e, pairs)


def resume(first, x0, h0, e0, x, h, e, pairs):
    for rows in tiles():
        x[rows, :] = x0[rows, :]
        h[rows, :] = h0[rows, :]
        value = e0[rows, :]
        e[rows, :] = value
        put_split(pairs.at[first % 2], rows, value)


def chebyshev_middle(first, last, x0, h0, e0, scale, inverse, high, low, x, h, e, pairs):
    resume(first, x0, h0, e0, x, h, e, pairs)
    chebyshev_steps(first, last, scale, inverse, high, low, x, h, e, pairs)


def fold_kernel(place, kept, came1, came2, came3, came4, away, keep):
    own = pl.ds(pl.multiple_of((place[1] % 2) * PIECE, PIECE), PIECE)
    other = pl.ds(pl.multiple_of((1 - place[1] % 2) * PIECE, PIECE), PIECE)
    for rows, target in (
        (other, away),
        (own, keep.at[:PIECE]),
        (slice(CHUNK, CHUNK + EXTRA), keep.at[PIECE:]),
    ):
        target[...] = (kept[0, rows, :] + came1[0, rows, :]) + (
            came2[0, rows, :] + came3[0, rows, :] + came4[0, rows, :]
        )


def chebyshev_last(
    with_groups, first, peers, groups, scale, inverse, high, low, x0, h0, e0, half, came,
    y, send, h, e, pairs,
):
    resume(first, x0, h0, e0, y, h, e, pairs)
    chebyshev_steps(first, DEGREE - 1, scale, inverse, high, low, y, h, e, pairs)
    y[...] += e[...]
    piece = half[:PIECE, :] + came[...]
    tail = half[PIECE:, :]
    if with_groups:
        lanes = lax.broadcasted_iota(jnp.int32, (EXTRA, RHS), 1)
        tail = jnp.zeros((EXTRA, RHS), F32)
        for corner in range(NCB):
            group = groups[0, corner].astype(F32)
            tail = jnp.where(lanes == corner, group, tail)
    for slot in range(NB):
        send[slot, :PIECE, :] = piece
        send[slot, PIECE:HEAD, :] = tail
        send[slot, HEAD:, :] = jnp.zeros((2 * BLOCK, RHS), F32)
    for turn in range(ROUNDS):
        send[peers[0, turn], HEAD:, :] = y[turn * 2 * BLOCK : (turn + 1) * 2 * BLOCK, :]


def gather_kernel(received, chunk, dots):
    for half in range(2):
        value = received[half, :PIECE, :]
        for slot in range(half + 2, NB, 2):
            value = value + received[slot, :PIECE, :]
        chunk[half * PIECE : (half + 1) * PIECE, :] = value
    value = received[0, PIECE:HEAD, :]
    for slot in range(1, NB):
        value = value + received[slot, PIECE:HEAD, :]
    dots[...] = value


def column_dot(pairs_of):
    total = None
    for first, second in pairs_of:
        part = jnp.sum(
            (first * second).reshape(first.shape[0] // 8, 8, RHS), axis=0
        )
        total = part if total is None else total + part
    return jnp.sum(total, axis=0, keepdims=True)


def apply_all(
    groups, place, peers, counts, others, received, y, totals, cih, cil, high, low, scale,
    m, n, coarse, pair,
):
    for apart, chunk in zip(APART, totals, strict=True):
        first = pl.multiple_of((place[0] ^ apart) * CHUNK, CHUNK)
        coarse[pl.ds(first, CHUNK), :] = chunk[...]
    for rows in tiles():
        put_split(pair, rows, coarse[rows, :])
    for rows in tiles():
        coarse[rows, :] = product(cih, cil, pair, rows)

    def block_of(group):
        return coarse[pl.ds(pl.multiple_of(group * BLOCK, BLOCK), BLOCK), :]

    half = (NB - NCB) * BLOCK
    m[:half, :] = y[:half, :]
    for corner in range(NCB):
        rows = slice(half + corner * BLOCK, half + (corner + 1) * BLOCK)
        m[rows, :] = y[rows, :] + block_of(groups[0, corner])
    for rows in tiles():
        put_split(pair, rows, m[rows, :])
    for rows in tiles():
        n[rows, :] = scale[rows, :] * m[rows, :] + product(high, low, pair, rows)
    for block in range(2 * ROUNDS):
        turn, side = block // 2, block % 2
        rows = slice(block * BLOCK, (block + 1) * BLOCK)
        first = HEAD + side * BLOCK
        other = received[peers[0, turn], first : first + BLOCK, :]
        if block >= NB - NCB:
            other = other + block_of(others[0, block - (NB - NCB)])
        n[rows, :] += jnp.where(side < counts[0, turn], m[rows, :] - other, 0.0)


def stage0_kernel(
    groups, place, peers, counts, received, y, t0, t1, t2, t3, t4, t5, t6, t7, cih, cil, high,
    low, scale, b,
    u, w, away, keep, others, coarse, pair, bins,
):
    totals = (t0, t1, t2, t3, t4, t5, t6, t7)
    lanes = lax.broadcasted_iota(jnp.int32, (1, RHS), 1)
    for corner in range(NCB):
        row = received[peers[0, (NB - NCB + corner) // 2], PIECE : PIECE + 1, :]
        picked = jnp.sum(jnp.where(lanes == corner, row, 0.0))
        others[0, corner] = picked.astype(jnp.int32)
    apply_all(
        groups, place, peers, counts, others, received, y, totals, cih, cil, high, low, scale,
        u, w, coarse, pair,
    )
    energy = column_dot([(b[r, :], u[r, :]) for r in tiles()])
    curve = column_dot([(w[r, :], u[r, :]) for r in tiles()])
    extra = jnp.concatenate([energy, curve, jnp.zeros((EXTRA - 2, RHS), F32)], axis=0)
    restrict_into(groups, place, w, extra, bins, away, keep)


def stage1_kernel(
    groups, place, peers, counts, others, received, y, t0, t1, t2, t3, t4, t5, t6, t7, cih, cil,
    high, low, scale, b, dots, u0, w0,
    m, n, u, w, away, keep, scalars, coarse, pair, bins,
):
    totals = (t0, t1, t2, t3, t4, t5, t6, t7)
    apply_all(
        groups, place, peers, counts, others, received, y, totals, cih, cil, high, low, scale,
        m, n, coarse, pair,
    )
    energy, curve = dots[0:1, :], dots[1:2, :]
    step = energy / curve
    scalars[...] = jnp.concatenate(
        [energy, curve, step, jnp.zeros((EXTRA - 3, RHS), F32)], axis=0
    )
    for r in tiles():
        u[r, :] = u0[r, :] - step * m[r, :]
        w[r, :] = w0[r, :] - step * n[r, :]
    new_energy = column_dot([(b[r, :] - step * w0[r, :], u[r, :]) for r in tiles()])
    new_curve = column_dot([(w[r, :], u[r, :]) for r in tiles()])
    cross = column_dot(
        [(u[r, :], w0[r, :]) for r in tiles()] + [(u0[r, :], w[r, :]) for r in tiles()]
    )
    extra = jnp.concatenate(
        [new_energy, new_curve, cross, jnp.zeros((EXTRA - 3, RHS), F32)], axis=0
    )
    restrict_into(groups, place, w, extra, bins, away, keep)


def stage2_kernel(
    groups, place, peers, counts, others, received, y, t0, t1, t2, t3, t4, t5, t6, t7, cih, cil,
    high, low, scale, b, dots, before, u0, w0, m0, n0, u1, w1,
    p, s, u, w, last, scalars, m, n, coarse, pair,
):
    totals = (t0, t1, t2, t3, t4, t5, t6, t7)
    apply_all(
        groups, place, peers, counts, others, received, y, totals, cih, cil, high, low, scale,
        m, n, coarse, pair,
    )
    energy0, curve0, step0 = before[0:1, :], before[1:2, :], before[2:3, :]
    energy, delta, cross = dots[0:1, :], dots[1:2, :], dots[2:3, :]
    beta = energy / energy0
    curve = delta + beta * cross + beta * beta * curve0
    step = energy / curve
    scalars[...] = jnp.concatenate(
        [energy, curve, step, step0, jnp.zeros((EXTRA - 4, RHS), F32)], axis=0
    )
    for r in tiles():
        p[r, :] = u1[r, :] + beta * u0[r, :]
        s[r, :] = w1[r, :] + beta * w0[r, :]
        u[r, :] = u1[r, :] - step * (m[r, :] + beta * m0[r, :])
        w[r, :] = w1[r, :] - step * (n[r, :] + beta * n0[r, :])
    new_energy = column_dot(
        [((b[r, :] - step0 * w0[r, :]) - step * s[r, :], u[r, :]) for r in tiles()]
    )
    new_curve = column_dot([(w[r, :], u[r, :]) for r in tiles()])
    cross = column_dot(
        [(u[r, :], s[r, :]) for r in tiles()] + [(p[r, :], w[r, :]) for r in tiles()]
    )
    for slot in range(last.shape[0]):
        last[slot, 0:1, :] = new_energy
        last[slot, 1:2, :] = new_curve
        last[slot, 2:3, :] = cross


def finish_kernel(all_dots, scalars, b, u0, w0, p, s, u, w, solution, residual):
    value = jnp.sum(all_dots[...], axis=0)
    energy, delta, cross = value[0:1, :], value[1:2, :], value[2:3, :]
    before, curve0 = scalars[0:1, :], scalars[1:2, :]
    step1, step0 = scalars[2:3, :], scalars[3:4, :]
    beta = energy / before
    step = energy / (delta + beta * cross + beta * beta * curve0)
    along = step1 + step * beta
    for r in tiles():
        solution[r, :] = step0 * u0[r, :] + along * p[r, :] + step * u[r, :]
        residual[r, :] = (
            (b[r, :] - step0 * w0[r, :]) - along * s[r, :] - step * w[r, :]
        )


APART = (0, 2, 4, 6, 1, 3, 5, 7)
FIELD = ((DOF, RHS), F32)
MATRIX = ((DOF, DOF), BF16)
HALF_BINS = ((4, CHUNK + EXTRA, RHS), F32)
SMALL = ((EXTRA, RHS), F32)
PAIR = pltpu.VMEM((DOF, 2 * RHS), BF16)
PAIRS = pltpu.VMEM((2, DOF, 2 * RHS), BF16)
FIELD_SCRATCH = pltpu.VMEM((DOF, RHS), F32)
BINS = pltpu.VMEM((NCB, CHUNK + EXTRA, RHS), F32)
STEP_FLOPS = 2 * DOF * DOF * RHS * 3


def on_device(
    right_side,
    diagonal,
    stiffness,
    column_index,
    neighbours,
    face_count,
    corner_group,
    coarse_inverse,
):
    corners = lax.axis_size("corner")
    devices = corners * lax.axis_size("sub")
    b = right_side.reshape(DOF, RHS)
    subs = lax.axis_size("sub")
    place = jnp.stack([lax.axis_index("corner"), lax.axis_index("sub")]).astype(jnp.int32)
    whole_inverse = lax.all_gather(coarse_inverse, "corner", axis=0, tiled=True)
    scale = jnp.broadcast_to(diagonal.reshape(DOF, 1), (DOF, RHS))

    def exchange(array, bit):
        return lax.ppermute(array, "corner", [(i, i ^ bit) for i in range(corners)])

    def middle(first, last, state):
        return call(
            functools.partial(chebyshev_middle, first, last), f"chebyshev_{first}", "vvvvvvv",
            "vvv", [FIELD] * 3, [PAIRS], STEP_FLOPS * (last - first),
        )(*state, scale, inverse, high, low)

    def precondition(source, away, keep, with_groups):
        came1 = exchange(away, 1)
        state = call(
            functools.partial(chebyshev_first, CUTS[1]), "chebyshev_first", "vvvvv", "vvv",
            [FIELD] * 3, [PAIRS], STEP_FLOPS * CUTS[1],
        )(source, scale, inverse, high, low)
        rest = keep[1:] + came1[1:]
        rest, *state = lax.optimization_barrier((rest, *state))
        came2 = exchange(rest[1:2], 2)
        came3 = exchange(rest[0:1], 4)
        came4 = exchange(rest[2:3], 6)
        state = middle(CUTS[1], CUTS[2], state)
        away, half = call(
            fold_kernel, "fold", "svvvvv", "vv",
            [((PIECE, RHS), F32), ((PIECE + EXTRA, RHS), F32)],
        )(place, keep, came1, came2, came3, came4)
        away, *state = lax.optimization_barrier((away, *state))
        came = lax.ppermute(away, "sub", [(i, i ^ 1) for i in range(subs)])
        state = middle(CUTS[2], CUTS[3], state)
        y, send = call(
            functools.partial(chebyshev_last, with_groups, CUTS[3]), "chebyshev_last",
            "ssvvvvvvvvv", "vv", [FIELD, ((NB, SLOT, RHS), F32)],
            [FIELD_SCRATCH, FIELD_SCRATCH, PAIRS], STEP_FLOPS * (DEGREE - 1 - CUTS[3]),
        )(neighbours, corner_group, scale, inverse, high, low, *state, half, came)
        received = lax.all_to_all(send, "sub", 0, 0, tiled=True)
        chunk, dots = call(
            gather_kernel, "gather", "v", "vv", [((CHUNK, RHS), F32), SMALL]
        )(received)
        if with_groups:
            chunk, *_ = lax.optimization_barrier((chunk, cih, cil))
        near = [chunk] + [exchange(chunk, bits) for bits in (2, 4, 6)]
        totals = near + [exchange(part, 1) for part in near]
        return received, y, totals, dots

    high, low, inverse, away, keep = call(
        build_kernel, "build", "sssvvv", "vvvvv",
        [MATRIX, MATRIX, FIELD, HALF_BINS, HALF_BINS],
        [
            pltpu.VMEM((NB // 2, BW, BLOCK, 2 * BLOCK), F32),
            pltpu.VMEM((BLOCK, DOF), F32),
            pltpu.VMEM((BLOCK, DOF), F32),
            pltpu.SMEM((NB, BW), jnp.int32),
            BINS,
        ],
        STEP_FLOPS * 3,
    )(column_index, corner_group, place, stiffness, scale, b)
    cih, cil = call(split_kernel, "split", "v", "vv", [MATRIX, MATRIX])(whole_inverse)

    received, y, totals, _ = precondition(b, away, keep, True)
    u0, w0, away, keep, others = call(
        stage0_kernel, "stage0", "ssss" + "v" * 16, "vvvvs",
        [FIELD, FIELD, HALF_BINS, HALF_BINS, ((1, NCB), jnp.int32)],
        [FIELD_SCRATCH, PAIR, BINS], STEP_FLOPS * 2,
    )(
        corner_group, place, neighbours, face_count, received, y, *totals, cih, cil,
        high, low, scale, b,
    )
    received, y, totals, dots = precondition(w0, away, keep, False)
    m0, n0, u1, w1, away, keep, before = call(
        stage1_kernel, "stage1", "sssss" + "v" * 19, "vvvvvvv",
        [FIELD] * 4 + [HALF_BINS, HALF_BINS, SMALL],
        [FIELD_SCRATCH, PAIR, BINS], STEP_FLOPS * 2,
    )(
        corner_group, place, neighbours, face_count, others, received, y, *totals, cih, cil,
        high, low, scale, b, dots, u0, w0,
    )
    received, y, totals, dots = precondition(w1, away, keep, False)
    p, s, u2, w2, last, scalars = call(
        stage2_kernel, "stage2", "sssss" + "v" * 24, "vvvvvv",
        [FIELD] * 4 + [((devices, 3, RHS), F32), SMALL],
        [FIELD_SCRATCH, FIELD_SCRATCH, FIELD_SCRATCH, PAIR], STEP_FLOPS * 2,
    )(
        corner_group, place, neighbours, face_count, others, received, y, *totals, cih, cil,
        high, low, scale, b, dots, before, u0, w0, m0, n0, u1, w1,
    )
    all_dots = lax.all_to_all(last, ("sub", "corner"), 0, 0, tiled=True)
    solution, residual = call(
        finish_kernel, "finish", "vvvvvvvvv", "vv", [FIELD, FIELD]
    )(all_dots, scalars, b, u0, w0, p, s, u2, w2)
    return (solution.reshape(right_side.shape), residual.reshape(right_side.shape))


def solution(mesh):
    placed = (
        P(("sub", "corner"), None, None),
        P(("sub", "corner"), None),
        P(("sub", "corner"), None, None),
        P(("sub", "corner"), None),
        P(("sub", "corner"), None),
        P(("sub", "corner"), None),
        P(("sub", "corner"), None),
        P("corner", None),
    )
    return jax.shard_map(
        on_device,
        mesh=mesh,
        in_specs=placed,
        out_specs=(P(("sub", "corner"), None, None), P(("sub", "corner"), None, None)),
        check_vma=False,
    )
```

```python
import functools
import math

import jax
import jax.numpy as jnp
from jax import lax
from jax.experimental import pallas as pl
from jax.experimental.pallas import tpu as pltpu
from jax.sharding import PartitionSpec as P

F32 = jnp.float32
BF16 = jnp.bfloat16
BLOCK = 64
NB = 16
DOF = NB * BLOCK
RHS = 128
BW = 3
NG = 16
NCB = 8
ROUNDS = 8
DEGREE = 8
HALF_RANGE = 0.8
SIGMA = 1.0 / HALF_RANGE
CHUNK = 128
PIECE = CHUNK // 2
EXTRA = 8
HEAD = PIECE + EXTRA
SLOT = HEAD + 2 * BLOCK
TILE = 256
CUTS = (0, 1, 4, 6)
VMEM_ROOM = 3 * 1024 * 1024


def spec(kind):
    return pl.BlockSpec(memory_space=pltpu.SMEM if kind == "s" else pltpu.VMEM)


def nbytes(shape, dtype):
    lanes = -(-shape[-1] // 128) * 128
    rows = -(-shape[-2] // 8) * 8
    return math.prod(shape[:-2]) * rows * lanes * jnp.dtype(dtype).itemsize


def call(body, name, kinds, out_kinds, outs, scratch=(), flops=0):
    def run(*operands):
        vmem = [(a.shape, a.dtype) for a, k in zip(operands, kinds, strict=True) if k == "v"]
        vmem += [o for o, k in zip(outs, out_kinds, strict=True) if k == "v"]
        vmem += [(s.shape, s.dtype) for s in scratch]
        return pl.pallas_call(
            body,
            name=name,
            in_specs=[spec(k) for k in kinds],
            out_specs=tuple(spec(k) for k in out_kinds),
            out_shape=tuple(jax.ShapeDtypeStruct(s, t) for s, t in outs),
            scratch_shapes=list(scratch),
            compiler_params=pltpu.CompilerParams(
                vmem_limit_bytes=VMEM_ROOM + sum(nbytes(*v) for v in vmem)
            ),
            cost_estimate=pl.CostEstimate(
                flops=flops, bytes_accessed=4 * 1024 * 1024, transcendentals=0
            ),
        )(*operands)

    return run


def tiles():
    return [slice(i, i + TILE) for i in range(0, DOF, TILE)]


def put_split(pair, rows, value):
    high = value.astype(BF16)
    pair[rows, :RHS] = high
    pair[rows, RHS:] = (value - high.astype(F32)).astype(BF16)


def product(high, low, pair, rows):
    both = jnp.dot(high[rows, :], pair[...], preferred_element_type=F32)
    rest = jnp.dot(low[rows, :], pair[:, :RHS], preferred_element_type=F32)
    return both[:, :RHS] + (both[:, RHS:] + rest)


def build_kernel(
    column, groups, place, stiffness, scale, b,
    high, low, inverse, away, keep, turned, even, odd, source, bins,
):
    restrict_into(groups, place, b, None, bins, away, keep)
    lane_half = lax.broadcasted_iota(jnp.int32, (BLOCK, 2 * BLOCK), 1) // BLOCK
    for pair in range(NB // 2):
        tile = stiffness[2 * pair : 2 * pair + 2]
        first = tile[:, :, : 2 * BLOCK].reshape(2 * BLOCK, 2 * BLOCK).T
        turned[pair, 0] = first[:BLOCK]
        turned[pair, 1] = first[BLOCK:]
        turned[pair, 2] = tile[:, :, 2 * BLOCK :].reshape(2 * BLOCK, BLOCK).T
    for row in range(NB):
        for link in range(BW):
            source[column[row, link], link] = row
    for row in range(NB):
        panel = odd if row % 2 else even
        panel[...] = jnp.zeros_like(panel)
        tile = stiffness[row, :, : 2 * BLOCK]
        swapped = pltpu.roll(tile, BLOCK, 1)
        last = stiffness[row, :, 2 * BLOCK :]
        twice = (
            jnp.where(lane_half == 0, tile, swapped),
            jnp.where(lane_half == 1, tile, swapped),
            jnp.concatenate([last, last], axis=1),
        )
        for link in range(BW):
            origin = source[row, link]
            for column_block, block in (
                (column[row, link], twice[link]),
                (origin, turned[origin // 2, link]),
            ):
                lanes = pl.ds(
                    pl.multiple_of((column_block // 2) * 2 * BLOCK, 2 * BLOCK), 2 * BLOCK
                )
                panel[:, lanes] += jnp.where(lane_half == column_block % 2, block, 0.0)
        rows = slice(row * BLOCK, (row + 1) * BLOCK)
        value = panel[...]
        top = value.astype(BF16)
        high[rows, :] = top
        low[rows, :] = (value - top.astype(F32)).astype(BF16)
    inverse[...] = 1.0 / scale[...]


def split_kernel(place, p0, p1, p2, p3, p4, p5, p6, p7, high, low):
    for apart, block in zip(APART, (p0, p1, p2, p3, p4, p5, p6, p7), strict=True):
        rows = pl.ds(pl.multiple_of((place[0] ^ apart) * CHUNK, CHUNK), CHUNK)
        value = block[...]
        top = value.astype(BF16)
        high[rows, :] = top
        low[rows, :] = (value - top.astype(F32)).astype(BF16)


def restrict_into(groups, place, vector, extra, bins, away, keep):
    bins[...] = jnp.zeros_like(bins)
    for corner in range(NCB):
        group = groups[0, corner]
        apart = (group // 2) ^ place[0]
        slot = (apart & 1) * 4 + (apart & 2) + ((apart >> 2) & 1)
        rows = pl.ds(pl.multiple_of((group % 2) * BLOCK, BLOCK), BLOCK)
        first = (NB - NCB + corner) * BLOCK
        bins[slot, rows, :] += vector[first : first + BLOCK, :]
    if extra is not None:
        for slot in range(NCB):
            bins[slot, CHUNK:, :] = extra
    keep[...] = bins[:4]
    away[...] = bins[4:]


def chebyshev_steps(first, last, scale, inverse, high, low, x, h, e, pairs):
    ratio = 1.0 / SIGMA
    for step in range(last):
        later = 1.0 / (2.0 * SIGMA - ratio)
        if step >= first:
            for rows in tiles():
                now = e[rows, :]
                image = product(high, low, pairs.at[step % 2], rows)
                x[rows, :] = now if step == 0 else x[rows, :] + now
                left = h[rows, :] - (scale[rows, :] * now + image)
                h[rows, :] = left
                new = (later * ratio) * now + (2.0 * later / HALF_RANGE) * (
                    left * inverse[rows, :]
                )
                e[rows, :] = new
                if step + 1 < last:
                    put_split(pairs.at[(step + 1) % 2], rows, new)
        ratio = later


def chebyshev_first(last, source, scale, inverse, high, low, x, h, e, pairs):
    for rows in tiles():
        value = source[rows, :]
        h[rows, :] = value
        value = value * inverse[rows, :]
        e[rows, :] = value
        put_split(pairs.at[0], rows, value)
    chebyshev_steps(0, last, scale, inverse, high, low, x, h, e, pairs)


def resume(first, x0, h0, e0, x, h, e, pairs):
    for rows in tiles():
        x[rows, :] = x0[rows, :]
        h[rows, :] = h0[rows, :]
        value = e0[rows, :]
        e[rows, :] = value
        put_split(pairs.at[first % 2], rows, value)


def chebyshev_middle(first, last, x0, h0, e0, scale, inverse, high, low, x, h, e, pairs):
    resume(first, x0, h0, e0, x, h, e, pairs)
    chebyshev_steps(first, last, scale, inverse, high, low, x, h, e, pairs)


def fold_kernel(place, kept, came1, came2, came3, came4, away, keep):
    own = pl.ds(pl.multiple_of((place[1] % 2) * PIECE, PIECE), PIECE)
    other = pl.ds(pl.multiple_of((1 - place[1] % 2) * PIECE, PIECE), PIECE)
    for rows, target in (
        (other, away),
        (own, keep.at[:PIECE]),
        (slice(CHUNK, CHUNK + EXTRA), keep.at[PIECE:]),
    ):
        target[...] = (kept[0, rows, :] + came1[0, rows, :]) + (
            came2[0, rows, :] + came3[0, rows, :] + came4[0, rows, :]
        )


def chebyshev_last(
    with_groups, first, peers, groups, scale, inverse, high, low, x0, h0, e0, half, came,
    y, send, h, e, pairs,
):
    resume(first, x0, h0, e0, y, h, e, pairs)
    chebyshev_steps(first, DEGREE - 1, scale, inverse, high, low, y, h, e, pairs)
    y[...] += e[...]
    piece = half[:PIECE, :] + came[...]
    tail = half[PIECE:, :]
    if with_groups:
        lanes = lax.broadcasted_iota(jnp.int32, (EXTRA, RHS), 1)
        tail = jnp.zeros((EXTRA, RHS), F32)
        for corner in range(NCB):
            group = groups[0, corner].astype(F32)
            tail = jnp.where(lanes == corner, group, tail)
    for slot in range(NB):
        send[slot, :PIECE, :] = piece
        send[slot, PIECE:HEAD, :] = tail
        send[slot, HEAD:, :] = jnp.zeros((2 * BLOCK, RHS), F32)
    for turn in range(ROUNDS):
        send[peers[0, turn], HEAD:, :] = y[turn * 2 * BLOCK : (turn + 1) * 2 * BLOCK, :]


def gather_kernel(received, chunk, dots):
    for half in range(2):
        value = received[half, :PIECE, :]
        for slot in range(half + 2, NB, 2):
            value = value + received[slot, :PIECE, :]
        chunk[half * PIECE : (half + 1) * PIECE, :] = value
    value = received[0, PIECE:HEAD, :]
    for slot in range(1, NB):
        value = value + received[slot, PIECE:HEAD, :]
    dots[...] = value


def column_dot(pairs_of):
    total = None
    for first, second in pairs_of:
        part = jnp.sum(
            (first * second).reshape(first.shape[0] // 8, 8, RHS), axis=0
        )
        total = part if total is None else total + part
    return jnp.sum(total, axis=0, keepdims=True)


def apply_all(
    groups, place, peers, counts, others, received, y, totals, cih, cil, high, low, scale,
    m, n, coarse, pair,
):
    for apart, chunk in zip(APART, totals, strict=True):
        first = pl.multiple_of((place[0] ^ apart) * CHUNK, CHUNK)
        coarse[pl.ds(first, CHUNK), :] = chunk[...]
    for rows in tiles():
        put_split(pair, rows, coarse[rows, :])
    for rows in tiles():
        coarse[rows, :] = product(cih, cil, pair, rows)

    def block_of(group):
        return coarse[pl.ds(pl.multiple_of(group * BLOCK, BLOCK), BLOCK), :]

    half = (NB - NCB) * BLOCK
    m[:half, :] = y[:half, :]
    for corner in range(NCB):
        rows = slice(half + corner * BLOCK, half + (corner + 1) * BLOCK)
        m[rows, :] = y[rows, :] + block_of(groups[0, corner])
    for rows in tiles():
        put_split(pair, rows, m[rows, :])
    for rows in tiles():
        n[rows, :] = scale[rows, :] * m[rows, :] + product(high, low, pair, rows)
    for block in range(2 * ROUNDS):
        turn, side = block // 2, block % 2
        rows = slice(block * BLOCK, (block + 1) * BLOCK)
        first = HEAD + side * BLOCK
        other = received[peers[0, turn], first : first + BLOCK, :]
        if block >= NB - NCB:
            other = other + block_of(others[0, block - (NB - NCB)])
        n[rows, :] += jnp.where(side < counts[0, turn], m[rows, :] - other, 0.0)


def stage0_kernel(
    groups, place, peers, counts, received, y, t0, t1, t2, t3, t4, t5, t6, t7, cih, cil, high,
    low, scale, b,
    u, w, away, keep, others, coarse, pair, bins,
):
    totals = (t0, t1, t2, t3, t4, t5, t6, t7)
    lanes = lax.broadcasted_iota(jnp.int32, (1, RHS), 1)
    for corner in range(NCB):
        row = received[peers[0, (NB - NCB + corner) // 2], PIECE : PIECE + 1, :]
        picked = jnp.sum(jnp.where(lanes == corner, row, 0.0))
        others[0, corner] = picked.astype(jnp.int32)
    apply_all(
        groups, place, peers, counts, others, received, y, totals, cih, cil, high, low, scale,
        u, w, coarse, pair,
    )
    energy = column_dot([(b[r, :], u[r, :]) for r in tiles()])
    curve = column_dot([(w[r, :], u[r, :]) for r in tiles()])
    extra = jnp.concatenate([energy, curve, jnp.zeros((EXTRA - 2, RHS), F32)], axis=0)
    restrict_into(groups, place, w, extra, bins, away, keep)


def stage1_kernel(
    groups, place, peers, counts, others, received, y, t0, t1, t2, t3, t4, t5, t6, t7, cih, cil,
    high, low, scale, b, dots, u0, w0,
    m, n, u, w, away, keep, scalars, coarse, pair, bins,
):
    totals = (t0, t1, t2, t3, t4, t5, t6, t7)
    apply_all(
        groups, place, peers, counts, others, received, y, totals, cih, cil, high, low, scale,
        m, n, coarse, pair,
    )
    energy, curve = dots[0:1, :], dots[1:2, :]
    step = energy / curve
    scalars[...] = jnp.concatenate(
        [energy, curve, step, jnp.zeros((EXTRA - 3, RHS), F32)], axis=0
    )
    for r in tiles():
        u[r, :] = u0[r, :] - step * m[r, :]
        w[r, :] = w0[r, :] - step * n[r, :]
    new_energy = column_dot([(b[r, :] - step * w0[r, :], u[r, :]) for r in tiles()])
    new_curve = column_dot([(w[r, :], u[r, :]) for r in tiles()])
    cross = column_dot(
        [(u[r, :], w0[r, :]) for r in tiles()] + [(u0[r, :], w[r, :]) for r in tiles()]
    )
    extra = jnp.concatenate(
        [new_energy, new_curve, cross, jnp.zeros((EXTRA - 3, RHS), F32)], axis=0
    )
    restrict_into(groups, place, w, extra, bins, away, keep)


def stage2_kernel(
    groups, place, peers, counts, others, received, y, t0, t1, t2, t3, t4, t5, t6, t7, cih, cil,
    high, low, scale, b, dots, before, u0, w0, m0, n0, u1, w1,
    p, s, u, w, last, scalars, m, n, coarse, pair,
):
    totals = (t0, t1, t2, t3, t4, t5, t6, t7)
    apply_all(
        groups, place, peers, counts, others, received, y, totals, cih, cil, high, low, scale,
        m, n, coarse, pair,
    )
    energy0, curve0, step0 = before[0:1, :], before[1:2, :], before[2:3, :]
    energy, delta, cross = dots[0:1, :], dots[1:2, :], dots[2:3, :]
    beta = energy / energy0
    curve = delta + beta * cross + beta * beta * curve0
    step = energy / curve
    scalars[...] = jnp.concatenate(
        [energy, curve, step, step0, jnp.zeros((EXTRA - 4, RHS), F32)], axis=0
    )
    for r in tiles():
        p[r, :] = u1[r, :] + beta * u0[r, :]
        s[r, :] = w1[r, :] + beta * w0[r, :]
        u[r, :] = u1[r, :] - step * (m[r, :] + beta * m0[r, :])
        w[r, :] = w1[r, :] - step * (n[r, :] + beta * n0[r, :])
    new_energy = column_dot(
        [((b[r, :] - step0 * w0[r, :]) - step * s[r, :], u[r, :]) for r in tiles()]
    )
    new_curve = column_dot([(w[r, :], u[r, :]) for r in tiles()])
    cross = column_dot(
        [(u[r, :], s[r, :]) for r in tiles()] + [(p[r, :], w[r, :]) for r in tiles()]
    )
    for slot in range(last.shape[0]):
        last[slot, 0:1, :] = new_energy
        last[slot, 1:2, :] = new_curve
        last[slot, 2:3, :] = cross


def finish_kernel(all_dots, scalars, b, u0, w0, p, s, u, w, solution, residual):
    value = jnp.sum(all_dots[...], axis=0)
    energy, delta, cross = value[0:1, :], value[1:2, :], value[2:3, :]
    before, curve0 = scalars[0:1, :], scalars[1:2, :]
    step1, step0 = scalars[2:3, :], scalars[3:4, :]
    beta = energy / before
    step = energy / (delta + beta * cross + beta * beta * curve0)
    along = step1 + step * beta
    for r in tiles():
        solution[r, :] = step0 * u0[r, :] + along * p[r, :] + step * u[r, :]
        residual[r, :] = (
            (b[r, :] - step0 * w0[r, :]) - along * s[r, :] - step * w[r, :]
        )


APART = (0, 2, 4, 6, 1, 3, 5, 7)
FIELD = ((DOF, RHS), F32)
MATRIX = ((DOF, DOF), BF16)
HALF_BINS = ((4, CHUNK + EXTRA, RHS), F32)
SMALL = ((EXTRA, RHS), F32)
PAIR = pltpu.VMEM((DOF, 2 * RHS), BF16)
PAIRS = pltpu.VMEM((2, DOF, 2 * RHS), BF16)
FIELD_SCRATCH = pltpu.VMEM((DOF, RHS), F32)
BINS = pltpu.VMEM((NCB, CHUNK + EXTRA, RHS), F32)
STEP_FLOPS = 2 * DOF * DOF * RHS * 3


def on_device(
    right_side,
    diagonal,
    stiffness,
    column_index,
    neighbours,
    face_count,
    corner_group,
    coarse_inverse,
):
    corners = lax.axis_size("corner")
    devices = corners * lax.axis_size("sub")
    b = right_side.reshape(DOF, RHS)
    subs = lax.axis_size("sub")
    place = jnp.stack([lax.axis_index("corner"), lax.axis_index("sub")]).astype(jnp.int32)
    scale = jnp.broadcast_to(diagonal.reshape(DOF, 1), (DOF, RHS))

    def exchange(array, bit):
        return lax.ppermute(array, "corner", [(i, i ^ bit) for i in range(corners)])

    def middle(first, last, state):
        return call(
            functools.partial(chebyshev_middle, first, last), f"chebyshev_{first}", "vvvvvvv",
            "vvv", [FIELD] * 3, [PAIRS], STEP_FLOPS * (last - first),
        )(*state, scale, inverse, high, low)

    def precondition(source, away, keep, bulk):
        came1 = exchange(away, 1)
        state = call(
            functools.partial(chebyshev_first, CUTS[1]), "chebyshev_first", "vvvvv", "vvv",
            [FIELD] * 3, [PAIRS], STEP_FLOPS * CUTS[1],
        )(source, scale, inverse, high, low)
        rest = keep[1:] + came1[1:]
        rest, *state = lax.optimization_barrier((rest, *state))
        came2 = exchange(rest[1:2], 2)
        came3 = exchange(rest[0:1], 4)
        came4 = exchange(rest[2:3], 6)
        state = middle(CUTS[1], CUTS[2], state)
        away, half = call(
            fold_kernel, "fold", "svvvvv", "vv",
            [((PIECE, RHS), F32), ((PIECE + EXTRA, RHS), F32)],
        )(place, keep, came1, came2, came3, came4)
        away, *state = lax.optimization_barrier((away, *state))
        came = lax.ppermute(away, "sub", [(i, i ^ 1) for i in range(subs)])
        parts = None
        if bulk is not None:
            bulk, *state = lax.optimization_barrier((bulk, *state))
            parts = [bulk] + [exchange(bulk, bits) for bits in (2, 4, 6)]
        state = middle(CUTS[2], CUTS[3], state)
        y, send = call(
            functools.partial(chebyshev_last, bulk is not None, CUTS[3]), "chebyshev_last",
            "ssvvvvvvvvv", "vv", [FIELD, ((NB, SLOT, RHS), F32)],
            [FIELD_SCRATCH, FIELD_SCRATCH, PAIRS], STEP_FLOPS * (DEGREE - 1 - CUTS[3]),
        )(neighbours, corner_group, scale, inverse, high, low, *state, half, came)
        received = lax.all_to_all(send, "sub", 0, 0, tiled=True)
        chunk, dots = call(
            gather_kernel, "gather", "v", "vv", [((CHUNK, RHS), F32), SMALL]
        )(received)
        if bulk is not None:
            chunk, *parts = lax.optimization_barrier((chunk, *parts))
        near = [chunk] + [exchange(chunk, bits) for bits in (2, 4, 6)]
        totals = near + [exchange(part, 1) for part in near]
        if bulk is not None:
            parts = parts + [exchange(part, 1) for part in parts]
        return received, y, totals, dots, parts

    high, low, inverse, away, keep = call(
        build_kernel, "build", "sssvvv", "vvvvv",
        [MATRIX, MATRIX, FIELD, HALF_BINS, HALF_BINS],
        [
            pltpu.VMEM((NB // 2, BW, BLOCK, 2 * BLOCK), F32),
            pltpu.VMEM((BLOCK, DOF), F32),
            pltpu.VMEM((BLOCK, DOF), F32),
            pltpu.SMEM((NB, BW), jnp.int32),
            BINS,
        ],
        STEP_FLOPS * 3,
    )(column_index, corner_group, place, stiffness, scale, b)
    received, y, totals, _, parts = precondition(b, away, keep, coarse_inverse)
    cih, cil = call(
        split_kernel, "split", "s" + "v" * 8, "vv", [MATRIX, MATRIX]
    )(place, *parts)
    u0, w0, away, keep, others = call(
        stage0_kernel, "stage0", "ssss" + "v" * 16, "vvvvs",
        [FIELD, FIELD, HALF_BINS, HALF_BINS, ((1, NCB), jnp.int32)],
        [FIELD_SCRATCH, PAIR, BINS], STEP_FLOPS * 2,
    )(
        corner_group, place, neighbours, face_count, received, y, *totals, cih, cil,
        high, low, scale, b,
    )
    received, y, totals, dots, _ = precondition(w0, away, keep, None)
    m0, n0, u1, w1, away, keep, before = call(
        stage1_kernel, "stage1", "sssss" + "v" * 19, "vvvvvvv",
        [FIELD] * 4 + [HALF_BINS, HALF_BINS, SMALL],
        [FIELD_SCRATCH, PAIR, BINS], STEP_FLOPS * 2,
    )(
        corner_group, place, neighbours, face_count, others, received, y, *totals, cih, cil,
        high, low, scale, b, dots, u0, w0,
    )
    received, y, totals, dots, _ = precondition(w1, away, keep, None)
    p, s, u2, w2, last, scalars = call(
        stage2_kernel, "stage2", "sssss" + "v" * 24, "vvvvvv",
        [FIELD] * 4 + [((devices, 3, RHS), F32), SMALL],
        [FIELD_SCRATCH, FIELD_SCRATCH, FIELD_SCRATCH, PAIR], STEP_FLOPS * 2,
    )(
        corner_group, place, neighbours, face_count, others, received, y, *totals, cih, cil,
        high, low, scale, b, dots, before, u0, w0, m0, n0, u1, w1,
    )
    all_dots = lax.all_to_all(last, ("sub", "corner"), 0, 0, tiled=True)
    solution, residual = call(
        finish_kernel, "finish", "vvvvvvvvv", "vv", [FIELD, FIELD]
    )(all_dots, scalars, b, u0, w0, p, s, u2, w2)
    return (solution.reshape(right_side.shape), residual.reshape(right_side.shape))


def solution(mesh):
    placed = (
        P(("sub", "corner"), None, None),
        P(("sub", "corner"), None),
        P(("sub", "corner"), None, None),
        P(("sub", "corner"), None),
        P(("sub", "corner"), None),
        P(("sub", "corner"), None),
        P(("sub", "corner"), None),
        P("corner", None),
    )
    return jax.shard_map(
        on_device,
        mesh=mesh,
        in_specs=placed,
        out_specs=(P(("sub", "corner"), None, None), P(("sub", "corner"), None, None)),
        check_vma=False,
    )
```

```python
import functools
import math

import jax
import jax.numpy as jnp
from jax import lax
from jax.experimental import pallas as pl
from jax.experimental.pallas import tpu as pltpu
from jax.sharding import PartitionSpec as P

F32 = jnp.float32
BF16 = jnp.bfloat16
BLOCK = 64
NB = 16
DOF = NB * BLOCK
RHS = 128
BW = 3
NG = 16
NCB = 8
ROUNDS = 8
DEGREE = 8
HALF_RANGE = 0.8
SIGMA = 1.0 / HALF_RANGE
CHUNK = 128
PIECE = CHUNK // 2
EXTRA = 8
HEAD = PIECE + EXTRA
SLOT = HEAD + 2 * BLOCK
TILE = 256
CUTS = (0, 1, 4, 6)
FULL = 5
VMEM_ROOM = 3 * 1024 * 1024


def spec(kind):
    return pl.BlockSpec(memory_space=pltpu.SMEM if kind == "s" else pltpu.VMEM)


def nbytes(shape, dtype):
    lanes = -(-shape[-1] // 128) * 128
    rows = -(-shape[-2] // 8) * 8
    return math.prod(shape[:-2]) * rows * lanes * jnp.dtype(dtype).itemsize


def call(body, name, kinds, out_kinds, outs, scratch=(), flops=0):
    def run(*operands):
        vmem = [(a.shape, a.dtype) for a, k in zip(operands, kinds, strict=True) if k == "v"]
        vmem += [o for o, k in zip(outs, out_kinds, strict=True) if k == "v"]
        vmem += [(s.shape, s.dtype) for s in scratch]
        return pl.pallas_call(
            body,
            name=name,
            in_specs=[spec(k) for k in kinds],
            out_specs=tuple(spec(k) for k in out_kinds),
            out_shape=tuple(jax.ShapeDtypeStruct(s, t) for s, t in outs),
            scratch_shapes=list(scratch),
            compiler_params=pltpu.CompilerParams(
                vmem_limit_bytes=VMEM_ROOM + sum(nbytes(*v) for v in vmem)
            ),
            cost_estimate=pl.CostEstimate(
                flops=flops, bytes_accessed=4 * 1024 * 1024, transcendentals=0
            ),
        )(*operands)

    return run


def tiles():
    return [slice(i, i + TILE) for i in range(0, DOF, TILE)]


def put_split(pair, rows, value):
    high = value.astype(BF16)
    pair[rows, :RHS] = high
    pair[rows, RHS:] = (value - high.astype(F32)).astype(BF16)


def product(high, low, pair, rows):
    both = jnp.dot(high[rows, :], pair[...], preferred_element_type=F32)
    if low is None:
        return both[:, :RHS] + both[:, RHS:]
    rest = jnp.dot(low[rows, :], pair[:, :RHS], preferred_element_type=F32)
    return both[:, :RHS] + (both[:, RHS:] + rest)


def build_kernel(
    column, groups, place, stiffness, scale, b,
    high, low, inverse, away, keep, turned, even, odd, source, bins,
):
    restrict_into(groups, place, b, None, bins, away, keep)
    lane_half = lax.broadcasted_iota(jnp.int32, (BLOCK, 2 * BLOCK), 1) // BLOCK
    for pair in range(NB // 2):
        tile = stiffness[2 * pair : 2 * pair + 2]
        first = tile[:, :, : 2 * BLOCK].reshape(2 * BLOCK, 2 * BLOCK).T
        turned[pair, 0] = first[:BLOCK]
        turned[pair, 1] = first[BLOCK:]
        turned[pair, 2] = tile[:, :, 2 * BLOCK :].reshape(2 * BLOCK, BLOCK).T
    for row in range(NB):
        for link in range(BW):
            source[column[row, link], link] = row
    for row in range(NB):
        panel = odd if row % 2 else even
        panel[...] = jnp.zeros_like(panel)
        tile = stiffness[row, :, : 2 * BLOCK]
        swapped = pltpu.roll(tile, BLOCK, 1)
        last = stiffness[row, :, 2 * BLOCK :]
        twice = (
            jnp.where(lane_half == 0, tile, swapped),
            jnp.where(lane_half == 1, tile, swapped),
            jnp.concatenate([last, last], axis=1),
        )
        for link in range(BW):
            origin = source[row, link]
            for column_block, block in (
                (column[row, link], twice[link]),
                (origin, turned[origin // 2, link]),
            ):
                lanes = pl.ds(
                    pl.multiple_of((column_block // 2) * 2 * BLOCK, 2 * BLOCK), 2 * BLOCK
                )
                panel[:, lanes] += jnp.where(lane_half == column_block % 2, block, 0.0)
        rows = slice(row * BLOCK, (row + 1) * BLOCK)
        value = panel[...]
        top = value.astype(BF16)
        high[rows, :] = top
        low[rows, :] = (value - top.astype(F32)).astype(BF16)
    inverse[...] = 1.0 / scale[...]


def split_kernel(place, p0, p1, p2, p3, p4, p5, p6, p7, high, low):
    for apart, block in zip(APART, (p0, p1, p2, p3, p4, p5, p6, p7), strict=True):
        rows = pl.ds(pl.multiple_of((place[0] ^ apart) * CHUNK, CHUNK), CHUNK)
        value = block[...]
        top = value.astype(BF16)
        high[rows, :] = top
        low[rows, :] = (value - top.astype(F32)).astype(BF16)


def restrict_into(groups, place, vector, extra, bins, away, keep):
    bins[...] = jnp.zeros_like(bins)
    for corner in range(NCB):
        group = groups[0, corner]
        apart = (group // 2) ^ place[0]
        slot = (apart & 1) * 4 + (apart & 2) + ((apart >> 2) & 1)
        rows = pl.ds(pl.multiple_of((group % 2) * BLOCK, BLOCK), BLOCK)
        first = (NB - NCB + corner) * BLOCK
        bins[slot, rows, :] += vector[first : first + BLOCK, :]
    if extra is not None:
        for slot in range(NCB):
            bins[slot, CHUNK:, :] = extra
    keep[...] = bins[:4]
    away[...] = bins[4:]


def chebyshev_steps(first, last, scale, inverse, high, low, x, h, e, pairs):
    ratio = 1.0 / SIGMA
    for step in range(last):
        later = 1.0 / (2.0 * SIGMA - ratio)
        if step >= first:
            for rows in tiles():
                now = e[rows, :]
                image = product(high, low if step < FULL else None, pairs.at[step % 2], rows)
                x[rows, :] = now if step == 0 else x[rows, :] + now
                left = h[rows, :] - (scale[rows, :] * now + image)
                h[rows, :] = left
                new = (later * ratio) * now + (2.0 * later / HALF_RANGE) * (
                    left * inverse[rows, :]
                )
                e[rows, :] = new
                if step + 1 < last:
                    put_split(pairs.at[(step + 1) % 2], rows, new)
        ratio = later


def chebyshev_first(last, source, scale, inverse, high, low, x, h, e, pairs):
    for rows in tiles():
        value = source[rows, :]
        h[rows, :] = value
        value = value * inverse[rows, :]
        e[rows, :] = value
        put_split(pairs.at[0], rows, value)
    chebyshev_steps(0, last, scale, inverse, high, low, x, h, e, pairs)


def resume(first, x0, h0, e0, x, h, e, pairs):
    for rows in tiles():
        x[rows, :] = x0[rows, :]
        h[rows, :] = h0[rows, :]
        value = e0[rows, :]
        e[rows, :] = value
        put_split(pairs.at[first % 2], rows, value)


def chebyshev_middle(first, last, x0, h0, e0, scale, inverse, high, low, x, h, e, pairs):
    resume(first, x0, h0, e0, x, h, e, pairs)
    chebyshev_steps(first, last, scale, inverse, high, low, x, h, e, pairs)


def fold_kernel(place, kept, came1, came2, came3, came4, away, keep):
    own = pl.ds(pl.multiple_of((place[1] % 2) * PIECE, PIECE), PIECE)
    other = pl.ds(pl.multiple_of((1 - place[1] % 2) * PIECE, PIECE), PIECE)
    for rows, target in (
        (other, away),
        (own, keep.at[:PIECE]),
        (slice(CHUNK, CHUNK + EXTRA), keep.at[PIECE:]),
    ):
        target[...] = (kept[0, rows, :] + came1[0, rows, :]) + (
            came2[0, rows, :] + came3[0, rows, :] + came4[0, rows, :]
        )


def chebyshev_last(
    with_groups, first, peers, groups, scale, inverse, high, low, x0, h0, e0, half, came,
    y, send, h, e, pairs,
):
    resume(first, x0, h0, e0, y, h, e, pairs)
    chebyshev_steps(first, DEGREE - 1, scale, inverse, high, low, y, h, e, pairs)
    y[...] += e[...]
    piece = half[:PIECE, :] + came[...]
    tail = half[PIECE:, :]
    if with_groups:
        lanes = lax.broadcasted_iota(jnp.int32, (EXTRA, RHS), 1)
        tail = jnp.zeros((EXTRA, RHS), F32)
        for corner in range(NCB):
            group = groups[0, corner].astype(F32)
            tail = jnp.where(lanes == corner, group, tail)
    for slot in range(NB):
        send[slot, :PIECE, :] = piece
        send[slot, PIECE:HEAD, :] = tail
        send[slot, HEAD:, :] = jnp.zeros((2 * BLOCK, RHS), F32)
    for turn in range(ROUNDS):
        send[peers[0, turn], HEAD:, :] = y[turn * 2 * BLOCK : (turn + 1) * 2 * BLOCK, :]


def gather_kernel(received, chunk, dots):
    for half in range(2):
        value = received[half, :PIECE, :]
        for slot in range(half + 2, NB, 2):
            value = value + received[slot, :PIECE, :]
        chunk[half * PIECE : (half + 1) * PIECE, :] = value
    value = received[0, PIECE:HEAD, :]
    for slot in range(1, NB):
        value = value + received[slot, PIECE:HEAD, :]
    dots[...] = value


def column_dot(pairs_of):
    total = None
    for first, second in pairs_of:
        part = jnp.sum(
            (first * second).reshape(first.shape[0] // 8, 8, RHS), axis=0
        )
        total = part if total is None else total + part
    return jnp.sum(total, axis=0, keepdims=True)


def apply_all(
    groups, place, peers, counts, others, received, y, totals, cih, cil, high, low, scale,
    m, n, coarse, pair,
):
    for apart, chunk in zip(APART, totals, strict=True):
        first = pl.multiple_of((place[0] ^ apart) * CHUNK, CHUNK)
        coarse[pl.ds(first, CHUNK), :] = chunk[...]
    for rows in tiles():
        put_split(pair, rows, coarse[rows, :])
    for rows in tiles():
        coarse[rows, :] = product(cih, cil, pair, rows)

    def block_of(group):
        return coarse[pl.ds(pl.multiple_of(group * BLOCK, BLOCK), BLOCK), :]

    half = (NB - NCB) * BLOCK
    m[:half, :] = y[:half, :]
    for corner in range(NCB):
        rows = slice(half + corner * BLOCK, half + (corner + 1) * BLOCK)
        m[rows, :] = y[rows, :] + block_of(groups[0, corner])
    for rows in tiles():
        put_split(pair, rows, m[rows, :])
    for rows in tiles():
        n[rows, :] = scale[rows, :] * m[rows, :] + product(high, low, pair, rows)
    for block in range(2 * ROUNDS):
        turn, side = block // 2, block % 2
        rows = slice(block * BLOCK, (block + 1) * BLOCK)
        first = HEAD + side * BLOCK
        other = received[peers[0, turn], first : first + BLOCK, :]
        if block >= NB - NCB:
            other = other + block_of(others[0, block - (NB - NCB)])
        n[rows, :] += jnp.where(side < counts[0, turn], m[rows, :] - other, 0.0)


def stage0_kernel(
    groups, place, peers, counts, received, y, t0, t1, t2, t3, t4, t5, t6, t7, cih, cil, high,
    low, scale, b,
    u, w, away, keep, others, coarse, pair, bins,
):
    totals = (t0, t1, t2, t3, t4, t5, t6, t7)
    lanes = lax.broadcasted_iota(jnp.int32, (1, RHS), 1)
    for corner in range(NCB):
        row = received[peers[0, (NB - NCB + corner) // 2], PIECE : PIECE + 1, :]
        picked = jnp.sum(jnp.where(lanes == corner, row, 0.0))
        others[0, corner] = picked.astype(jnp.int32)
    apply_all(
        groups, place, peers, counts, others, received, y, totals, cih, cil, high, low, scale,
        u, w, coarse, pair,
    )
    energy = column_dot([(b[r, :], u[r, :]) for r in tiles()])
    curve = column_dot([(w[r, :], u[r, :]) for r in tiles()])
    extra = jnp.concatenate([energy, curve, jnp.zeros((EXTRA - 2, RHS), F32)], axis=0)
    restrict_into(groups, place, w, extra, bins, away, keep)


def stage1_kernel(
    groups, place, peers, counts, others, received, y, t0, t1, t2, t3, t4, t5, t6, t7, cih, cil,
    high, low, scale, b, dots, u0, w0,
    m, n, u, w, away, keep, scalars, coarse, pair, bins,
):
    totals = (t0, t1, t2, t3, t4, t5, t6, t7)
    apply_all(
        groups, place, peers, counts, others, received, y, totals, cih, cil, high, low, scale,
        m, n, coarse, pair,
    )
    energy, curve = dots[0:1, :], dots[1:2, :]
    step = energy / curve
    scalars[...] = jnp.concatenate(
        [energy, curve, step, jnp.zeros((EXTRA - 3, RHS), F32)], axis=0
    )
    for r in tiles():
        u[r, :] = u0[r, :] - step * m[r, :]
        w[r, :] = w0[r, :] - step * n[r, :]
    new_energy = column_dot([(b[r, :] - step * w0[r, :], u[r, :]) for r in tiles()])
    new_curve = column_dot([(w[r, :], u[r, :]) for r in tiles()])
    cross = column_dot(
        [(u[r, :], w0[r, :]) for r in tiles()] + [(u0[r, :], w[r, :]) for r in tiles()]
    )
    extra = jnp.concatenate(
        [new_energy, new_curve, cross, jnp.zeros((EXTRA - 3, RHS), F32)], axis=0
    )
    restrict_into(groups, place, w, extra, bins, away, keep)


def stage2_kernel(
    groups, place, peers, counts, others, received, y, t0, t1, t2, t3, t4, t5, t6, t7, cih, cil,
    high, low, scale, b, dots, before, u0, w0, m0, n0, u1, w1,
    p, s, u, w, last, scalars, m, n, coarse, pair,
):
    totals = (t0, t1, t2, t3, t4, t5, t6, t7)
    apply_all(
        groups, place, peers, counts, others, received, y, totals, cih, cil, high, low, scale,
        m, n, coarse, pair,
    )
    energy0, curve0, step0 = before[0:1, :], before[1:2, :], before[2:3, :]
    energy, delta, cross = dots[0:1, :], dots[1:2, :], dots[2:3, :]
    beta = energy / energy0
    curve = delta + beta * cross + beta * beta * curve0
    step = energy / curve
    scalars[...] = jnp.concatenate(
        [energy, curve, step, step0, jnp.zeros((EXTRA - 4, RHS), F32)], axis=0
    )
    for r in tiles():
        p[r, :] = u1[r, :] + beta * u0[r, :]
        s[r, :] = w1[r, :] + beta * w0[r, :]
        u[r, :] = u1[r, :] - step * (m[r, :] + beta * m0[r, :])
        w[r, :] = w1[r, :] - step * (n[r, :] + beta * n0[r, :])
    new_energy = column_dot(
        [((b[r, :] - step0 * w0[r, :]) - step * s[r, :], u[r, :]) for r in tiles()]
    )
    new_curve = column_dot([(w[r, :], u[r, :]) for r in tiles()])
    cross = column_dot(
        [(u[r, :], s[r, :]) for r in tiles()] + [(p[r, :], w[r, :]) for r in tiles()]
    )
    for slot in range(last.shape[0]):
        last[slot, 0:1, :] = new_energy
        last[slot, 1:2, :] = new_curve
        last[slot, 2:3, :] = cross


def finish_kernel(all_dots, scalars, b, u0, w0, p, s, u, w, solution, residual):
    value = jnp.sum(all_dots[...], axis=0)
    energy, delta, cross = value[0:1, :], value[1:2, :], value[2:3, :]
    before, curve0 = scalars[0:1, :], scalars[1:2, :]
    step1, step0 = scalars[2:3, :], scalars[3:4, :]
    beta = energy / before
    step = energy / (delta + beta * cross + beta * beta * curve0)
    along = step1 + step * beta
    for r in tiles():
        solution[r, :] = step0 * u0[r, :] + along * p[r, :] + step * u[r, :]
        residual[r, :] = (
            (b[r, :] - step0 * w0[r, :]) - along * s[r, :] - step * w[r, :]
        )


APART = (0, 2, 4, 6, 1, 3, 5, 7)
FIELD = ((DOF, RHS), F32)
MATRIX = ((DOF, DOF), BF16)
HALF_BINS = ((4, CHUNK + EXTRA, RHS), F32)
SMALL = ((EXTRA, RHS), F32)
PAIR = pltpu.VMEM((DOF, 2 * RHS), BF16)
PAIRS = pltpu.VMEM((2, DOF, 2 * RHS), BF16)
FIELD_SCRATCH = pltpu.VMEM((DOF, RHS), F32)
BINS = pltpu.VMEM((NCB, CHUNK + EXTRA, RHS), F32)
STEP_FLOPS = 2 * DOF * DOF * RHS * 3


def on_device(
    right_side,
    diagonal,
    stiffness,
    column_index,
    neighbours,
    face_count,
    corner_group,
    coarse_inverse,
):
    corners = lax.axis_size("corner")
    devices = corners * lax.axis_size("sub")
    b = right_side.reshape(DOF, RHS)
    subs = lax.axis_size("sub")
    place = jnp.stack([lax.axis_index("corner"), lax.axis_index("sub")]).astype(jnp.int32)
    scale = jnp.broadcast_to(diagonal.reshape(DOF, 1), (DOF, RHS))

    def exchange(array, bit):
        return lax.ppermute(array, "corner", [(i, i ^ bit) for i in range(corners)])

    def middle(first, last, state):
        return call(
            functools.partial(chebyshev_middle, first, last), f"chebyshev_{first}", "vvvvvvv",
            "vvv", [FIELD] * 3, [PAIRS], STEP_FLOPS * (last - first),
        )(*state, scale, inverse, high, low)

    def precondition(source, away, keep, bulk):
        came1 = exchange(away, 1)
        state = call(
            functools.partial(chebyshev_first, CUTS[1]), "chebyshev_first", "vvvvv", "vvv",
            [FIELD] * 3, [PAIRS], STEP_FLOPS * CUTS[1],
        )(source, scale, inverse, high, low)
        rest = keep[1:] + came1[1:]
        rest, *state = lax.optimization_barrier((rest, *state))
        came2 = exchange(rest[1:2], 2)
        came3 = exchange(rest[0:1], 4)
        came4 = exchange(rest[2:3], 6)
        state = middle(CUTS[1], CUTS[2], state)
        away, half = call(
            fold_kernel, "fold", "svvvvv", "vv",
            [((PIECE, RHS), F32), ((PIECE + EXTRA, RHS), F32)],
        )(place, keep, came1, came2, came3, came4)
        away, *state = lax.optimization_barrier((away, *state))
        came = lax.ppermute(away, "sub", [(i, i ^ 1) for i in range(subs)])
        parts = None
        if bulk is not None:
            bulk, *state = lax.optimization_barrier((bulk, *state))
            parts = [bulk] + [exchange(bulk, bits) for bits in (2, 4, 6)]
        state = middle(CUTS[2], CUTS[3], state)
        y, send = call(
            functools.partial(chebyshev_last, bulk is not None, CUTS[3]), "chebyshev_last",
            "ssvvvvvvvvv", "vv", [FIELD, ((NB, SLOT, RHS), F32)],
            [FIELD_SCRATCH, FIELD_SCRATCH, PAIRS], STEP_FLOPS * (DEGREE - 1 - CUTS[3]),
        )(neighbours, corner_group, scale, inverse, high, low, *state, half, came)
        received = lax.all_to_all(send, "sub", 0, 0, tiled=True)
        chunk, dots = call(
            gather_kernel, "gather", "v", "vv", [((CHUNK, RHS), F32), SMALL]
        )(received)
        near = [chunk] + [exchange(chunk, bits) for bits in (2, 4, 6)]
        if bulk is not None:
            near, parts = lax.optimization_barrier((near, parts))
        totals = near + [exchange(part, 1) for part in near]
        if bulk is not None:
            parts = parts + [exchange(part, 1) for part in parts]
        return received, y, totals, dots, parts

    high, low, inverse, away, keep = call(
        build_kernel, "build", "sssvvv", "vvvvv",
        [MATRIX, MATRIX, FIELD, HALF_BINS, HALF_BINS],
        [
            pltpu.VMEM((NB // 2, BW, BLOCK, 2 * BLOCK), F32),
            pltpu.VMEM((BLOCK, DOF), F32),
            pltpu.VMEM((BLOCK, DOF), F32),
            pltpu.SMEM((NB, BW), jnp.int32),
            BINS,
        ],
        STEP_FLOPS * 3,
    )(column_index, corner_group, place, stiffness, scale, b)
    received, y, totals, _, parts = precondition(b, away, keep, coarse_inverse)
    cih, cil = call(
        split_kernel, "split", "s" + "v" * 8, "vv", [MATRIX, MATRIX]
    )(place, *parts)
    u0, w0, away, keep, others = call(
        stage0_kernel, "stage0", "ssss" + "v" * 16, "vvvvs",
        [FIELD, FIELD, HALF_BINS, HALF_BINS, ((1, NCB), jnp.int32)],
        [FIELD_SCRATCH, PAIR, BINS], STEP_FLOPS * 2,
    )(
        corner_group, place, neighbours, face_count, received, y, *totals, cih, cil,
        high, low, scale, b,
    )
    received, y, totals, dots, _ = precondition(w0, away, keep, None)
    m0, n0, u1, w1, away, keep, before = call(
        stage1_kernel, "stage1", "sssss" + "v" * 19, "vvvvvvv",
        [FIELD] * 4 + [HALF_BINS, HALF_BINS, SMALL],
        [FIELD_SCRATCH, PAIR, BINS], STEP_FLOPS * 2,
    )(
        corner_group, place, neighbours, face_count, others, received, y, *totals, cih, cil,
        high, low, scale, b, dots, u0, w0,
    )
    received, y, totals, dots, _ = precondition(w1, away, keep, None)
    p, s, u2, w2, last, scalars = call(
        stage2_kernel, "stage2", "sssss" + "v" * 24, "vvvvvv",
        [FIELD] * 4 + [((devices, 3, RHS), F32), SMALL],
        [FIELD_SCRATCH, FIELD_SCRATCH, FIELD_SCRATCH, PAIR], STEP_FLOPS * 2,
    )(
        corner_group, place, neighbours, face_count, others, received, y, *totals, cih, cil,
        high, low, scale, b, dots, before, u0, w0, m0, n0, u1, w1,
    )
    all_dots = lax.all_to_all(last, ("sub", "corner"), 0, 0, tiled=True)
    solution, residual = call(
        finish_kernel, "finish", "vvvvvvvvv", "vv", [FIELD, FIELD]
    )(all_dots, scalars, b, u0, w0, p, s, u2, w2)
    return (solution.reshape(right_side.shape), residual.reshape(right_side.shape))


def solution(mesh):
    placed = (
        P(("sub", "corner"), None, None),
        P(("sub", "corner"), None),
        P(("sub", "corner"), None, None),
        P(("sub", "corner"), None),
        P(("sub", "corner"), None),
        P(("sub", "corner"), None),
        P(("sub", "corner"), None),
        P("corner", None),
    )
    return jax.shard_map(
        on_device,
        mesh=mesh,
        in_specs=placed,
        out_specs=(P(("sub", "corner"), None, None), P(("sub", "corner"), None, None)),
        check_vma=False,
    )
```
